32 devices in a mesh: seq: 8 (over z, y), head: 4 (over x, core).
Axes of the slice: x: 2, y: 2, z: 4, core: 2. Of those that a mesh axis runs over, the one named last changes fastest.
Arguments:
- queries: bfloat16 [256, 64, 128], P(None, 'head'), may hold values from -64 to 64
- keys: bfloat16 [512, 16, 8, 128], P('seq', None, 'head'), may hold values from -6 to 6
- values: bfloat16 [512, 16, 8, 128], P('seq', None, 'head'), may hold values from -6 to 6
- page_table: int32 [512], P('seq'), may hold values from 0 to 63, as said below
- offset: int32 [1], replicated, may hold values from 4096 to 7936
- conv_kernel: float32 [64, 6, 11], P('head'), may hold values from -0.6 to 1.6
- head_mix: float32 [64, 2], P('head'), may hold values from -0.8 to 1.8
- out_weight: bfloat16 [8192, 8192], P('head', 'seq'), may hold values from -0.0625 to 0.0625
Outputs:
- projected: bfloat16 [256, 8192], P('head', 'seq')
The draws below stay inside these ranges and needn't reach their ends.
Inputs may be any that keep to these rules, and one draw needn't show every extreme that they name: `page_table`: each aligned block of 64 entries that starts at a multiple of 64 is a permutation of 0 to 63.
All inputs are finite; a program needn't handle non-finite values.
Results may differ from the reference program's by a relative error of at most 0.02.
Values may be sent and summed in bfloat16 or wider, within the bound.
No kernel may reach another device: no remote copies, remote signals or barrier semaphores. Data moves between devices by JAX's collectives and lax.ppermute only.
A program may use at most 192 MiB of HBM per device.

```python
import jax
import jax.numpy as jnp
from jax import lax

H = 64
KVH = 8
DH = 128
D = 8192
HG = 2
CQ = 6
CK = 11
PAGE = 16
Q = 256
KEYS_DEV = 1024
PAGES_DEV = 64
KEYS = 8192
PAGES = 512


def place_pages(pages, order):
    return jnp.zeros_like(pages).at[order].set(pages)


def page_order(one_key):
    return jax.random.permutation(one_key, PAGES_DEV).astype(jnp.int32)


def shared_world(key):
    base = jax.random.fold_in(key, 11)
    streams = jax.random.split(base, 8)
    seq_devices = KEYS // KEYS_DEV
    logical = jnp.clip(jax.random.normal(streams[0], (KEYS, KVH, DH), jnp.float32), -6.0, 6.0)
    table = jax.vmap(page_order)(jax.random.split(streams[1], seq_devices))
    near = jax.random.randint(streams[2], (Q, H), 1, seq_devices - 4) * KEYS_DEV
    near = near + jax.random.randint(streams[3], (Q, H), -3, 3)
    spread_far = jax.random.randint(streams[4], (Q, H), 0, (seq_devices - 4) * KEYS_DEV)
    pick = jax.random.randint(streams[5], (Q, H), 0, 2)
    target = jnp.where(pick == 0, near, spread_far).astype(jnp.int32)
    kv_of_head = (jnp.arange(H, dtype=jnp.int32) // (H // KVH)).astype(jnp.int32)
    target_keys = logical[target, kv_of_head[None, :]]
    strength = jax.random.uniform(streams[6], (Q, H), jnp.float32, 0.9, 1.4)
    noise = jnp.clip(jax.random.normal(streams[7], (Q, H, DH), jnp.float32), -6.0, 6.0)
    queries = jnp.clip(noise + strength[:, :, None] * target_keys, -64.0, 64.0)
    return (logical, table, queries)


def draw_queries(key, part):
    return shared_world(key)[2].astype(jnp.bfloat16)


def draw_keys(key, part):
    logical, table, queries = shared_world(key)
    seq_devices = KEYS // KEYS_DEV
    paged = logical.reshape(seq_devices, PAGES_DEV, PAGE, KVH, DH)
    physical = jax.vmap(place_pages)(paged, table)
    return physical.reshape(PAGES, PAGE, KVH, DH).astype(jnp.bfloat16)


def draw_page_table(key, part):
    return shared_world(key)[1].reshape(PAGES).astype(jnp.int32)


def draw_conv_kernel(key, part):
    stream = jax.random.fold_in(key, 23)
    noise = jnp.clip(0.2 * jax.random.normal(stream, (H, CQ, CK), jnp.float32), -0.6, 0.6)
    centre = (jnp.arange(CQ)[:, None] == 0) & (jnp.arange(CK)[None, :] == (CK - 1) // 2)
    return noise + centre.astype(jnp.float32)[None]


def draw_head_mix(key, part):
    stream = jax.random.fold_in(key, 31)
    noise = jax.random.uniform(stream, (H, HG), jnp.float32, -0.6, 0.6)
    diagonal = jnp.arange(H)[:, None] % HG == jnp.arange(HG)[None, :]
    return noise + diagonal.astype(jnp.float32)


def level_of(own_key, extent, cuts, low, top_value):
    def one(dim, shards_of):
        heights = jax.random.uniform(jax.random.fold_in(jax.random.fold_in(own_key, 6), dim), (shards_of,), jnp.float32, low / len(cuts), top_value / len(cuts))
        return jnp.repeat(jnp.exp(heights), extent[dim] // shards_of).reshape((-1,) + (1,) * (len(extent) - dim - 1))

    factor_of = one(*cuts[0])
    for cut in cuts[1:]:
        factor_of = factor_of * one(*cut)
    return factor_of


def gaussian(key, shape, deviation, bound, cuts=(), kind=jnp.bfloat16):
    result = jax.random.normal(key, shape, jnp.float32) * deviation
    if len(cuts) > 0:
        result = level_of(key, shape, cuts, -0.22, 0.18) * result
    return jnp.clip(result, min=-bound, max=bound).astype(kind)


def setup_inputs(seed: int = 0) -> dict:
    splits = jax.random.split(jax.random.key(seed), 9)
    return {
        "queries": draw_queries(jax.random.fold_in(splits[8], 71), 0),
        "keys": draw_keys(jax.random.fold_in(splits[8], 71), 0),
        "values": gaussian(splits[2], (PAGES, PAGE, KVH, DH), 1.0, 6.0, ((0, 8), (2, 4))),
        "page_table": draw_page_table(jax.random.fold_in(splits[8], 71), 0),
        "offset": jax.random.randint(splits[4], (1,), KEYS - 4 * KEYS_DEV, KEYS - Q + 1).astype(jnp.int32),
        "conv_kernel": draw_conv_kernel(jax.random.fold_in(splits[8], 71), 0),
        "head_mix": draw_head_mix(jax.random.fold_in(splits[8], 71), 0),
        "out_weight": gaussian(splits[7], (H * DH, D), (H * DH) ** -0.5, 0.0625, ((0, 4), (1, 8))),
    }


NEGATIVE = -1.0e30


def reference(queries, keys, values, page_table, offset, conv_kernel, head_mix, out_weight):
    page_owner = jnp.arange(PAGES, dtype=jnp.int32) // PAGES_DEV
    physical = (page_owner * PAGES_DEV + page_table).astype(jnp.int32)
    logical_keys = jnp.take(keys, physical, axis=0).reshape(KEYS, KVH, DH)
    logical_values = jnp.take(values, physical, axis=0).reshape(KEYS, KVH, DH)
    query_pos = offset[0] + jnp.arange(Q, dtype=jnp.int32)
    key_pos = jnp.arange(KEYS, dtype=jnp.int32)
    visible = key_pos[None, :] <= query_pos[:, None]
    rim_width = (CK - 1) // 2
    per_kv = H // KVH
    scale = 1.0 / (DH ** 0.5)

    def one_group(group_id):
        first_head = (group_id * HG).astype(jnp.int32)
        heads = first_head + jnp.arange(HG, dtype=jnp.int32)
        kv_index = (heads // per_kv).astype(jnp.int32)
        group_q = lax.dynamic_slice_in_dim(queries, first_head, HG, 1).astype(jnp.float32)
        group_k = jnp.take(logical_keys, kv_index, axis=1).astype(jnp.float32)
        group_v = jnp.take(logical_values, kv_index, axis=1).astype(jnp.float32)
        scores = jnp.einsum("qgd,kgd->gqk", group_q, group_k, precision=lax.Precision.HIGHEST) * scale
        zeroed = jnp.where(visible[None], scores, 0.0)
        shifted = jnp.pad(zeroed, ((0, 0), (CQ - 1, 0), (rim_width, rim_width)))
        kernel = lax.dynamic_slice_in_dim(conv_kernel, first_head, HG, 0)
        convolved = jnp.zeros((HG, Q, KEYS), zeroed.dtype)
        for qtap in range(CQ):
            rows = shifted[:, CQ - 1 - qtap:CQ - 1 - qtap + Q, :]
            for ktap in range(CK):
                convolved = convolved + kernel[:, qtap, ktap][:, None, None] * rows[:, :, ktap:ktap + KEYS]
        mixing = lax.dynamic_slice_in_dim(head_mix, first_head, HG, 0)
        mixed = jnp.zeros_like(convolved)
        for source in range(HG):
            mixed = mixed + mixing[:, source][:, None, None] * convolved[source][None]
        masked = jnp.where(visible[None], mixed, NEGATIVE)
        peak = jnp.max(masked, axis=2)
        exps = jnp.where(visible[None], jnp.exp(masked - peak[:, :, None]), 0.0)
        total = jnp.sum(exps, axis=2)
        weights = exps.astype(jnp.bfloat16).astype(jnp.float32)
        summed = jnp.einsum("gqk,kgd->qgd", weights, group_v, precision=lax.Precision.HIGHEST)
        return (summed / total.T[:, :, None]).astype(jnp.bfloat16)

    grouped = lax.map(one_group, jnp.arange(H // HG, dtype=jnp.int32))
    attended = jnp.transpose(grouped, (1, 0, 2, 3)).reshape(Q, H * DH)
    return jnp.dot(attended, out_weight, preferred_element_type=jnp.float32).astype(jnp.bfloat16)
```

```python
import functools
import math

import jax
import jax.numpy as jnp
from jax import lax
from jax.experimental import pallas as pl
from jax.experimental.pallas import tpu as pltpu
from jax.sharding import PartitionSpec as P

NEG = -1e30
BF = jnp.bfloat16
F32 = jnp.float32
LANES = 128
BAND = 32
HEAD_PAD = 272
TAIL_PAD = 416
VPAD = 128
LOG2E = 1.4426950408889634


def nt(a, b, **kw):
    return lax.dot_general(a, b, (((1,), (1,)), ((), ())), preferred_element_type=F32, **kw)


def iota(shape, dim):
    return lax.broadcasted_iota(jnp.int32, shape, dim)


def skew(x, shift):
    return pltpu.roll(x, shift, 1, stride=1, stride_axis=0)


def pack_stats(lse, heads):
    hi = lse.astype(BF).astype(F32)
    mid = (lse - hi).astype(BF).astype(F32)
    low = lse - hi - mid
    return hi + pltpu.roll(mid, heads, 1) + pltpu.roll(low, 2 * heads, 1)


def unpack_stats(x, heads):
    x = x.astype(F32)
    return x + pltpu.roll(x, LANES - heads, 1) + pltpu.roll(x, LANES - 2 * heads, 1)


def attend_kernel(dims, kv, off_ref, table_ref, q_ref, k_ref, v_ref, left_ref, right_ref,
                  toep_ref, band_ref, keep_ref, send_ref,
                  kext, krot, kwrap, vext, khat, vhat, qhat, toep, s_ref, out, stat, fsc, msc):
    rows, heads, kvs, pages, page, qtaps, ktaps, keys_here, split_bit = dims
    hk = heads // kvs
    pairs = hk // 2
    rim = (ktaps - 1) // 2
    nblk = keys_here // LANES
    base = HEAD_PAD
    seq = lax.axis_index("seq")
    diag = off_ref[0] - seq * keys_here
    has_diag = (diag >= 1 - rows) & (diag <= keys_here + 8)
    shift = jnp.where(has_diag, lax.rem(diag + 2 * LANES, LANES), 0)

    kext[pl.ds(0, base - page), :] = jnp.zeros((base - page, LANES), F32)
    kext[pl.ds(base + keys_here + page, TAIL_PAD - page), :] = jnp.zeros((TAIL_PAD - page, LANES), F32)
    kext[pl.ds(base - page, page), :] = left_ref[pl.ds(kv, page, stride=kvs), :]
    kext[pl.ds(base + keys_here, page), :] = right_ref[pl.ds(kv, page, stride=kvs), :]
    vext[pl.ds(0, VPAD), :] = jnp.zeros((VPAD, LANES), F32)
    vext[pl.ds(VPAD + keys_here, VPAD), :] = jnp.zeros((VPAD, LANES), F32)
    for p in range(pages):
        src = table_ref[p] * (page * kvs) + kv
        kext[pl.ds(base + p * page, page), :] = k_ref[pl.ds(src, page, stride=kvs), :]
        vext[pl.ds(VPAD + p * page, page), :] = v_ref[pl.ds(src, page, stride=kvs), :]
    krot[...] = kext[pl.ds(base - 8 + shift, keys_here + 16), :]
    kwrap[...] = kext[pl.ds(base - 8 - LANES + shift, LANES + 16), :]
    first = iota((LANES, LANES), 0) < LANES - shift
    for n in range(nblk):
        for b in range(ktaps):
            part = krot[pl.ds(n * LANES + 8 + b - rim, LANES), :]
            if n == nblk - 1:
                part = jnp.where(first, part, kwrap[pl.ds(8 + b - rim, LANES), :])
            khat[pl.ds(n * LANES, LANES), b * LANES:(b + 1) * LANES] = part.astype(BF)
        part = vext[pl.ds(VPAD + n * LANES + shift, LANES), :]
        if n == nblk - 1:
            part = jnp.where(first, part, vext[pl.ds(shift, LANES), :])
        vhat[pl.ds(n * LANES, LANES), 0:LANES] = part.astype(BF)
    vhat[:, LANES:] = jnp.ones((keys_here, LANES), BF)

    def make_queries(p):
        per = ktaps * BAND
        for h in range(2):
            for b in range(ktaps):
                row = toep_ref[pl.ds((p * 2 + h) * ktaps + b, 1), :]
                t32 = skew(jnp.broadcast_to(row, (BAND, LANES)), 0)
                hi = t32.astype(BF)
                low = (t32 - hi.astype(F32)).astype(BF)
                at = h * per + b * BAND
                toep[pl.ds(at, BAND), 0:LANES] = hi
                toep[pl.ds(at, BAND), LANES:] = low
        for t in range(rows // (2 * BAND)):
            r0 = t * 2 * BAND
            halves = []
            for g in range(2):
                col = pl.multiple_of(((kv * pairs + p) * 2 + g) * LANES, LANES)
                two = q_ref[pl.ds(r0, 2 * BAND), pl.ds(col, LANES)]
                if t == 0:
                    one = jnp.concatenate([jnp.zeros((BAND, LANES), BF), two[:BAND]], axis=0)
                else:
                    one = q_ref[pl.ds(r0 - BAND, 2 * BAND), pl.ds(col, LANES)]
                halves.append(jnp.concatenate([one, two], axis=1))
            rhs = jnp.concatenate(halves + halves, axis=0)
            y = jnp.dot(toep[...], rhs, preferred_element_type=F32)
            for h in range(2):
                for b in range(ktaps):
                    at = h * per + b * BAND
                    for e in range(2):
                        qhat[h, pl.ds(r0 + e * BAND, BAND), b * LANES:(b + 1) * LANES] = (
                            y[at:at + BAND, e * LANES:(e + 1) * LANES].astype(BF))

    def finish(p, h, s):
        peak = jnp.max(s, axis=1, keepdims=True)
        w = jnp.exp2(s - peak).astype(BF)
        o = jnp.dot(w, vhat[...], preferred_element_type=F32)
        total = o[:, LANES:]
        head = p * 2 + h
        out[:, pl.ds(pl.multiple_of(head * LANES, LANES), LANES)] = (o[:, :LANES] / total).astype(BF)
        lse = peak + jnp.log2(total)
        stat[...] = jnp.where(iota((rows, LANES), 1) == head, lse, stat[...])

    stat[...] = jnp.zeros((rows, LANES), F32)

    @pl.when(diag > keys_here + 8)
    def _():
        def body(p, c):
            make_queries(p)
            for h in range(2):
                finish(p, h, nt(qhat[h], khat[...]))
            return c
        lax.fori_loop(0, pairs, body, 0)

    @pl.when(has_diag)
    def _():
        nwin = 3 * LANES
        win = kext[pl.ds(base + diag, nwin), :].astype(BF)
        flip = (iota((nwin, nwin), 0) + iota((nwin, nwin), 1) == nwin - 1).astype(F32).astype(BF)
        rev = jnp.dot(flip, win, preferred_element_type=F32).astype(BF)
        lane = iota((LANES, LANES), 1)
        row = iota((LANES, LANES), 0)
        future = (lane >= 127 - 10) & (lane <= 126)
        fsc[:, 0:8, :] = jnp.zeros((2, 8, LANES), F32)
        msc[...] = jnp.zeros((2, 2 * LANES, LANES), F32)
        block0 = (diag + 2 * LANES - shift) // LANES - 2

        def body(p, c):
            make_queries(p)
            for g in range(2):
                col = pl.multiple_of(((kv * pairs + p) * 2 + g) * LANES, LANES)
                w = nt(q_ref[:, pl.ds(col, LANES)], rev)
                for f in range(rows // LANES):
                    sub = w[f * LANES:(f + 1) * LANES]
                    near = skew(sub[:, (2 - f) * LANES:(3 - f) * LANES], 0)
                    far = skew(sub[:, (1 - f) * LANES:(2 - f) * LANES], 0)
                    both = jnp.where(row <= lane, near, far)
                    fsc[g, pl.ds(8 + f * LANES, LANES), :] = jnp.where(future, both, 0.0)
            tiles = [None, None]
            for g in range(2):
                for a in range(qtaps):
                    slot = qtaps * g + a
                    part = pltpu.roll(fsc[g, pl.ds(8 - a, rows), :], (16 * slot + 16) % LANES, 1)
                    i = slot // 8
                    tiles[i] = part if tiles[i] is None else tiles[i] + part
            fst = jnp.concatenate(tiles, axis=1)
            for h in range(2):
                taps = band_ref[p * 2 + h]
                for u in range(5, 15):
                    msc[h, pl.ds(u, 16, stride=16), :] = pltpu.roll(taps, 21 - u, 1)
            col_key = iota((1, keys_here), 1) + shift
            col_key = jnp.where(col_key >= keys_here, col_key - keys_here, col_key)
            visible = col_key <= diag + iota((rows, 1), 0)
            for h in range(2):
                s_ref[...] = nt(qhat[h], khat[...])
                corr = jnp.dot(fst, msc[h], preferred_element_type=F32, precision=lax.Precision.HIGHEST)
                for f in range(rows // LANES):
                    r = skew(corr[f * LANES:(f + 1) * LANES], 112)
                    for e in range(2):
                        y = lane - row + (16 if e else -112)
                        n = block0 - 1 + f + e
                        low = jnp.where(n == -1, LANES - shift, 0)
                        high = jnp.where(n == nblk - 1, LANES - shift, LANES)
                        high = jnp.where((n >= -1) & (n < nblk), high, 0)
                        at = jnp.where(n == -1, nblk - 1, jnp.clip(n, 0, nblk - 1))
                        ok = (y >= 7) & (y <= 16) & (lane >= low) & (lane < high)
                        where = (pl.ds(f * LANES, LANES), pl.ds(pl.multiple_of(at * LANES, LANES), LANES))
                        s_ref[where] = s_ref[where] - jnp.where(ok, r, 0.0)
                finish(p, h, jnp.where(visible, s_ref[...], NEG))
            return c
        lax.fori_loop(0, pairs, body, 0)

    @pl.when(diag < 1 - rows)
    def _():
        out[...] = jnp.zeros_like(out)
        stat[...] = jnp.where(iota((rows, LANES), 1) < hk, NEG, 0.0)

    half = rows // 2
    side = lax.rem(seq // split_bit, 2)
    stats = pack_stats(stat[...], hk)
    stat[...] = stats
    for ref, part in ((keep_ref, side), (send_ref, 1 - side)):
        at = pl.multiple_of(part * half, half)
        ref[:, :hk * LANES] = out[pl.ds(at, half), :]
        ref[:, hk * LANES:] = stat[pl.ds(at, half), :].astype(BF)


def attend(kv, offset, table, q2, k2, v2, left, right, toep_rows, band_rows, kvs, page, conv_shape):
    rows = q2.shape[0]
    heads, qtaps, ktaps = conv_shape
    hk = heads // kvs
    pages = table.shape[0]
    keys_here = pages * page
    dims = (rows, heads, kvs, pages, page, qtaps, ktaps, keys_here, 1)
    smem = pl.BlockSpec(memory_space=pltpu.SMEM)
    vmem = pl.BlockSpec(memory_space=pltpu.VMEM)
    width = hk * LANES + LANES
    shape = jax.ShapeDtypeStruct((rows // 2, width), BF)
    flops = 2 * hk * rows * keys_here * (ktaps + 2) * LANES
    return pl.pallas_call(
        functools.partial(attend_kernel, dims, kv),
        out_shape=(shape, shape),
        in_specs=[smem, smem] + [vmem] * 7,
        out_specs=(vmem, vmem),
        scratch_shapes=[
            pltpu.VMEM((HEAD_PAD + keys_here + TAIL_PAD, LANES), F32),
            pltpu.VMEM((keys_here + 16, LANES), F32),
            pltpu.VMEM((LANES + 16, LANES), F32),
            pltpu.VMEM((keys_here + 2 * VPAD, LANES), F32),
            pltpu.VMEM((keys_here, ktaps * LANES), BF),
            pltpu.VMEM((keys_here, 2 * LANES), BF),
            pltpu.VMEM((2, rows, ktaps * LANES), BF),
            pltpu.VMEM((2 * ktaps * BAND, 2 * LANES), BF),
            pltpu.VMEM((rows, keys_here), F32),
            pltpu.VMEM((rows, hk * LANES), BF),
            pltpu.VMEM((rows, LANES), F32),
            pltpu.VMEM((2, rows + 8, LANES), F32),
            pltpu.VMEM((2, 2 * LANES, LANES), F32),
        ],
        compiler_params=pltpu.CompilerParams(vmem_limit_bytes=40 * 2**20),
        cost_estimate=pl.CostEstimate(flops=flops, bytes_accessed=4 * 2**20, transcendentals=hk * rows * keys_here),
        name=f"attend{kv}",
    )(offset, table, q2, k2, v2, left, right, toep_rows, band_rows)


def merge_kernel(hk, bit, last, a_ref, b_ref, *rest):
    if last:
        (keep_ref,) = rest
    else:
        keep_ref, send_ref, buf = rest
    wide = hk * LANES
    la = unpack_stats(a_ref[:, wide:], hk)
    lb = unpack_stats(b_ref[:, wide:], hk)
    top = jnp.maximum(la, lb)
    lse = top + jnp.log2(jnp.exp2(la - top) + jnp.exp2(lb - top))
    wa = jnp.exp2(la - lse)
    wb = jnp.exp2(lb - lse)
    rows = a_ref.shape[0]
    for h in range(hk):
        cols = slice(h * LANES, (h + 1) * LANES)
        mixed = a_ref[:, cols].astype(F32) * wa[:, h:h + 1] + b_ref[:, cols].astype(F32) * wb[:, h:h + 1]
        if last:
            keep_ref[:, cols] = mixed.astype(BF)
        else:
            buf[:, cols] = mixed
    if not last:
        lse = jnp.where(iota((rows, LANES), 1) < hk, lse, 0.0)
        buf[:, wide:] = pack_stats(lse, hk)
        side = lax.rem(lax.axis_index("seq") // bit, 2)
        half = rows // 2
        keep_ref[...] = buf[pl.ds(pl.multiple_of(side * half, half), half), :].astype(BF)
        send_ref[...] = buf[pl.ds(pl.multiple_of((1 - side) * half, half), half), :].astype(BF)


def merge(a, b, hk, bit, last):
    rows, width = a.shape
    vmem = pl.BlockSpec(memory_space=pltpu.VMEM)
    if last:
        shapes = jax.ShapeDtypeStruct((rows, hk * LANES), BF)
        specs, scratch = vmem, []
    else:
        one = jax.ShapeDtypeStruct((rows // 2, width), BF)
        shapes, specs = (one, one), (vmem, vmem)
        scratch = [pltpu.VMEM((rows, width), F32)]
    return pl.pallas_call(
        functools.partial(merge_kernel, hk, bit, last),
        out_shape=shapes,
        in_specs=[vmem, vmem],
        out_specs=specs,
        scratch_shapes=scratch,
        cost_estimate=pl.CostEstimate(flops=4 * rows * width, bytes_accessed=6 * rows * width, transcendentals=rows * LANES * 5),
        name=f"merge{bit}",
    )(a, b)


def project_kernel(pieces, heads_axis, *refs):
    xs = refs[:pieces]
    w_ref, keep_ref, send_ref, xbuf = refs[pieces:]
    seq = lax.axis_index("seq")
    count = lax.axis_size("seq")
    bits = count.bit_length() - 1
    mine = 0
    for i in range(bits):
        mine = mine * 2 + lax.rem(seq // (1 << i), 2)
    rows = xbuf.shape[0]
    unit = rows // count
    per = pieces // (bits + 1)
    width = xs[0].shape[1]
    for c in range(pieces // (bits + 1)):
        cols = slice(c * width, (c + 1) * width)
        held = 0
        for x_ref in xs[c * (bits + 1):(c + 1) * (bits + 1)]:
            for k in range(x_ref.shape[0] // unit):
                to = jnp.bitwise_xor(mine, held)
                xbuf[pl.ds(pl.multiple_of(to * unit, unit), unit), cols] = x_ref[pl.ds(k * unit, unit), :].astype(xbuf.dtype)
                held += 1
    y = jnp.dot(xbuf[...].astype(BF), w_ref[...], preferred_element_type=F32)
    core = lax.rem(lax.axis_index("head"), 2)
    block = rows // heads_axis
    for g in range(heads_axis // 2):
        even = y[(2 * g) * block:(2 * g + 1) * block]
        odd = y[(2 * g + 1) * block:(2 * g + 2) * block]
        keep_ref[pl.ds(g * block, block), :] = jnp.where(core == 0, even, odd)
        send_ref[pl.ds(g * block, block), :] = jnp.where(core == 0, odd, even).astype(BF)


def project(pieces, weight, rows):
    heads_axis = lax.axis_size("head")
    vmem = pl.BlockSpec(memory_space=pltpu.VMEM)
    depth, cols = weight.shape
    unit = rows // lax.axis_size("seq")
    return pl.pallas_call(
        functools.partial(project_kernel, len(pieces), heads_axis),
        out_shape=(jax.ShapeDtypeStruct((rows // 2, cols), F32), jax.ShapeDtypeStruct((rows // 2, cols), BF)),
        in_specs=[vmem] * (len(pieces) + 1),
        out_specs=(vmem, vmem),
        scratch_shapes=[pltpu.VMEM((rows, depth), BF if unit % 16 == 0 else F32)],
        compiler_params=pltpu.CompilerParams(vmem_limit_bytes=40 * 2**20),
        cost_estimate=pl.CostEstimate(flops=2 * rows * depth * cols, bytes_accessed=2 * depth * cols, transcendentals=0),
        name="project",
    )(*pieces, weight)


def swap(x, axis, bit):
    count = lax.axis_size(axis)
    return lax.ppermute(x, axis, [(i, i ^ bit) for i in range(count)])


def per_device(queries, keys, values, page_table, offset, conv_kernel, head_mix, out_weight):
    rows, heads, head_dim = queries.shape
    pages, page, kvs, _ = keys.shape
    qtaps, ktaps = conv_kernel.shape[1:]
    group = head_mix.shape[1]
    hk = heads // kvs
    seq_count = lax.axis_size("seq")
    head_count = lax.axis_size("head")

    flat = pages * page * kvs
    ends = seq_count - 1

    def page_of(p):
        return lax.dynamic_slice_in_dim(keys, page_table[p], 1, 0).reshape(page * kvs, head_dim).astype(F32)

    left = lax.ppermute(page_of(pages - 1).astype(BF), "seq", [(i, i + 1) for i in range(ends)]).astype(F32)
    right = lax.ppermute(page_of(0).astype(BF), "seq", [(i + 1, i) for i in range(ends)]).astype(F32)

    k2 = keys.astype(F32).reshape(flat, head_dim)
    v2 = values.astype(F32).reshape(flat, head_dim)
    q2 = queries.reshape(rows, heads * head_dim)

    scale = LOG2E / math.sqrt(head_dim)
    taps = (head_mix * scale).reshape(heads // group, group, group, 1, 1) * conv_kernel.reshape(
        heads // group, 1, group, qtaps, ktaps)
    rows_t = jnp.flip(jnp.transpose(taps, (0, 1, 4, 2, 3)), 4)
    lead = BAND - (qtaps - 1)
    rows_t = jnp.pad(rows_t, ((0, 0),) * 4 + ((lead, 2 * BAND - lead - qtaps),)).reshape(heads * ktaps, 4 * BAND)
    band = jnp.flip(taps, 4)
    band = jnp.stack(
        [jnp.pad(band[:, :, :, a], ((0, 0),) * 3 + ((qtaps - 1 - a, LANES - ktaps - (qtaps - 1 - a)),)) for a in range(qtaps)],
        axis=3,
    ).reshape(heads, group * qtaps, LANES)
    band = jnp.pad(band, ((0, 0), (0, 16 - group * qtaps), (0, 0)))

    bits = [1 << i for i in range(seq_count.bit_length() - 1)]
    pieces = []
    for kv in range(kvs):
        toep_rows = rows_t[kv * hk * ktaps:(kv + 1) * hk * ktaps]
        band_rows = band[kv * hk:(kv + 1) * hk]
        keep, send = attend(kv, offset, page_table, q2, k2, v2, left, right, toep_rows, band_rows,
                            kvs, page, conv_kernel.shape)
        for i, bit in enumerate(bits):
            got = swap(send, "seq", bit)
            if i + 1 < len(bits):
                keep, send = merge(keep, got, hk, bits[i + 1], False)
            else:
                piece = merge(keep, got, hk, 0, True)
        held = [piece]
        for bit in reversed(bits):
            whole = held[0] if len(held) == 1 else jnp.concatenate(held, axis=0)
            held.append(swap(whole, "seq", bit))
        pieces += held

    keep, send = project(pieces, out_weight, rows)
    me = lax.axis_index("head")
    got = swap(send, "head", 1)
    total = keep + got.astype(F32)
    block = rows // head_count
    bit = 2
    while bit < head_count:
        parts = total.reshape(-1, 2, block, total.shape[1])
        high = (me // bit) % 2 == 1
        mine = jnp.where(high, parts[:, 1], parts[:, 0])
        other = jnp.where(high, parts[:, 0], parts[:, 1]).astype(BF)
        got = swap(other, "head", bit)
        total = (mine + got.astype(F32)).reshape(-1, total.shape[1])
        bit *= 2
    return total.astype(BF)


def solution(mesh):
    placed = (
        P(None, "head", None),
        P("seq", None, "head", None),
        P("seq", None, "head", None),
        P("seq"),
        P(),
        P("head", None, None),
        P("head", None),
        P("head", "seq"),
    )
    return jax.shard_map(
        per_device, mesh=mesh, in_specs=placed, out_specs=P("head", "seq"), check_vma=False
    )
```

```python
import functools
import math

import jax
import jax.numpy as jnp
from jax import lax
from jax.experimental import pallas as pl
from jax.experimental.pallas import tpu as pltpu
from jax.sharding import PartitionSpec as P

NEG = -1e30
BF = jnp.bfloat16
F32 = jnp.float32
LANES = 128
BAND = 32
HEAD_PAD = 272
TAIL_PAD = 416
VPAD = 128
LOG2E = 1.4426950408889634


def nt(a, b, **kw):
    return lax.dot_general(a, b, (((1,), (1,)), ((), ())), preferred_element_type=F32, **kw)


def iota(shape, dim):
    return lax.broadcasted_iota(jnp.int32, shape, dim)


def skew(x, shift):
    return pltpu.roll(x, shift, 1, stride=1, stride_axis=0)


def pack_stats(lse, heads):
    hi = lse.astype(BF).astype(F32)
    mid = (lse - hi).astype(BF).astype(F32)
    low = lse - hi - mid
    return hi + pltpu.roll(mid, heads, 1) + pltpu.roll(low, 2 * heads, 1)


def unpack_stats(x, heads):
    x = x.astype(F32)
    return x + pltpu.roll(x, LANES - heads, 1) + pltpu.roll(x, LANES - 2 * heads, 1)


def prepare_kernel(dims, table_ref, mix_ref, conv_ref, q_ref, k_ref, v_ref,
                   q2_ref, k2_ref, v2_ref, band_ref, *rest):
    rows, heads, kvs, pages, page, qtaps, ktaps = dims
    qhats, (q32, rows_sc, base_sc, *toeps) = rest[:kvs], rest[kvs:]
    pairs = heads // 2
    scale = LOG2E / math.sqrt(LANES)
    q32[...] = q_ref[...].reshape(rows * heads, LANES).astype(F32)
    for h in range(heads):
        q2_ref[:, h * LANES:(h + 1) * LANES] = q32[pl.ds(h, rows, stride=heads), :].astype(BF)
    conv = conv_ref[...]
    turned = jnp.swapaxes(conv, 0, 1)
    lane = iota((ktaps, LANES), 1)
    lane2 = iota((qtaps, LANES), 1) + iota((qtaps, LANES), 0)
    rows_all = []
    for h in range(heads):
        rows_all.append(sum(jnp.where(lane == BAND - a, conv[a][:, h:h + 1], 0.0) for a in range(qtaps)))
        base_sc[h] = sum(jnp.where(lane2 == 15 - b, turned[b][:, h:h + 1], 0.0) for b in range(ktaps))
    band_ref[...] = jnp.zeros_like(band_ref)
    for h in range(heads):
        for g in range(2):
            src = h // 2 * 2 + g
            band_ref[h, g * qtaps:(g + 1) * qtaps, :] = base_sc[src] * (mix_ref[g, h] * scale)
        rows_sc[h] = rows_all[h // 2 * 2] * (mix_ref[0, h] * scale) + pltpu.roll(
            rows_all[h // 2 * 2 + 1], 2 * BAND, 1) * (mix_ref[1, h] * scale)

    def make_queries(p, dst, head, toep):
        per = ktaps * BAND
        for h in range(2):
            for b in range(ktaps):
                t32 = skew(jnp.broadcast_to(rows_sc[2 * p + h, b:b + 1, :], (BAND, LANES)), 0)
                hi = t32.astype(BF)
                at = h * per + b * BAND
                toep[pl.ds(at, BAND), 0:LANES] = hi
                toep[pl.ds(at, BAND), LANES:] = (t32 - hi.astype(F32)).astype(BF)
        for t in range(rows // (2 * BAND)):
            r0 = t * 2 * BAND
            halves = []
            for g in range(2):
                where = pl.ds(pl.multiple_of((p * 2 + g) * LANES, LANES), LANES)
                two = q2_ref[pl.ds(r0, 2 * BAND), where]
                if t == 0:
                    one = jnp.concatenate([jnp.zeros((BAND, LANES), BF), two[:BAND]], axis=0)
                else:
                    one = q2_ref[pl.ds(r0 - BAND, 2 * BAND), where]
                halves.append(jnp.concatenate([one, two], axis=1))
            rhs = jnp.concatenate(halves + halves, axis=0)
            y = jnp.dot(toep[...], rhs, preferred_element_type=F32)
            for h in range(2):
                for b in range(ktaps):
                    for e in range(2):
                        at = h * per + b * BAND
                        dst[head + h, pl.ds(r0 + e * BAND, BAND), b * LANES:(b + 1) * LANES] = (
                            y[at:at + BAND, e * LANES:(e + 1) * LANES].astype(BF))

    for kv in range(kvs):
        each = pairs // kvs

        def body(i, c, kv=kv, each=each):
            for j, toep in enumerate(toeps):
                p = i * len(toeps) + j
                make_queries(kv * each + p, qhats[kv], 2 * p, toep)
            return c

        lax.fori_loop(0, each // len(toeps), body, 0)
    for p in range(pages):
        keys = k_ref[table_ref[p]].astype(F32)
        values = v_ref[table_ref[p]].astype(F32)
        for kv in range(kvs):
            k2_ref[kv, p * page:(p + 1) * page, :] = keys[:, kv, :]
            v2_ref[kv, p * page:(p + 1) * page, :] = values[:, kv, :]


def prepare(table, mix, conv, queries, keys, values):
    rows, heads, _ = queries.shape
    pages, page, kvs, _ = keys.shape
    qtaps, ktaps, _ = conv.shape
    smem = pl.BlockSpec(memory_space=pltpu.SMEM)
    vmem = pl.BlockSpec(memory_space=pltpu.VMEM)
    store = jax.ShapeDtypeStruct((kvs, pages * page, LANES), F32)
    toep = pltpu.VMEM((2 * ktaps * BAND, 2 * LANES), BF)
    return pl.pallas_call(
        functools.partial(prepare_kernel, (rows, heads, kvs, pages, page, qtaps, ktaps)),
        out_shape=(
            jax.ShapeDtypeStruct((rows, heads * LANES), BF),
            store,
            store,
            jax.ShapeDtypeStruct((heads, 16, LANES), F32),
        )
        + (jax.ShapeDtypeStruct((heads // kvs, rows, ktaps * LANES), BF),) * kvs,
        in_specs=[smem, smem] + [vmem] * 4,
        out_specs=(vmem,) * (4 + kvs),
        scratch_shapes=[
            pltpu.VMEM((rows * heads, LANES), F32),
            pltpu.VMEM((heads, ktaps, LANES), F32),
            pltpu.VMEM((heads, qtaps, LANES), F32),
            toep,
            toep,
        ],
        compiler_params=pltpu.CompilerParams(vmem_limit_bytes=26 * 2**20),
        cost_estimate=pl.CostEstimate(flops=heads * rows * ktaps * LANES * 256 * 2, bytes_accessed=16 * 2**20, transcendentals=0),
        name="prepare",
    )(table, mix, conv, queries, keys, values)


def attend_kernel(dims, kv, off_ref, qhat_ref, q_ref, k_ref, v_ref, left_ref, right_ref,
                  band_ref, keep_ref, send_ref,
                  kext, krot, kwrap, vext, khat, vhat, sa, sb, ca, cb, out, stat, rev, fsc, fst, msc):
    rows, heads, kvs, page, qtaps, ktaps, keys_here, split_bit = dims
    hk = heads // kvs
    pairs = hk // 2
    rim = (ktaps - 1) // 2
    nblk = keys_here // LANES
    base = HEAD_PAD
    seq = lax.axis_index("seq")
    diag = off_ref[0] - seq * keys_here
    has_diag = (diag >= 1 - rows) & (diag <= keys_here + 8)
    shift = jnp.where(has_diag, lax.rem(diag + 2 * LANES, LANES), 0)

    kext[pl.ds(0, base - page), :] = jnp.zeros((base - page, LANES), F32)
    kext[pl.ds(base + keys_here + page, TAIL_PAD - page), :] = jnp.zeros((TAIL_PAD - page, LANES), F32)
    kext[pl.ds(base - page, page), :] = left_ref[:, kv, :].astype(F32)
    kext[pl.ds(base + keys_here, page), :] = right_ref[:, kv, :].astype(F32)
    kext[pl.ds(base, keys_here), :] = k_ref[kv]
    vext[pl.ds(0, VPAD), :] = jnp.zeros((VPAD, LANES), F32)
    vext[pl.ds(VPAD + keys_here, VPAD), :] = jnp.zeros((VPAD, LANES), F32)
    vext[pl.ds(VPAD, keys_here), :] = v_ref[kv]
    krot[...] = kext[pl.ds(base - 8 + shift, keys_here + 16), :]
    kwrap[...] = kext[pl.ds(base - 8 - LANES + shift, LANES + 16), :]
    first = iota((LANES, LANES), 0) < LANES - shift
    for n in range(nblk):
        for b in range(ktaps):
            part = krot[pl.ds(n * LANES + 8 + b - rim, LANES), :]
            if n == nblk - 1:
                part = jnp.where(first, part, kwrap[pl.ds(8 + b - rim, LANES), :])
            khat[pl.ds(n * LANES, LANES), b * LANES:(b + 1) * LANES] = part.astype(BF)
        part = vext[pl.ds(VPAD + n * LANES + shift, LANES), :]
        if n == nblk - 1:
            part = jnp.where(first, part, vext[pl.ds(shift, LANES), :])
        vhat[pl.ds(n * LANES, LANES), 0:LANES] = part.astype(BF)
    vhat[:, LANES:] = jnp.ones((keys_here, LANES), BF)

    cols = 2 * LANES
    nwin = 3 * LANES
    lane = iota((LANES, LANES), 1)
    row = iota((LANES, LANES), 0)
    block0 = (diag + 2 * LANES - shift) // LANES - 2

    def q_cols(p, g):
        return pl.ds(pl.multiple_of(((kv * pairs + p) * 2 + g) * LANES, LANES), LANES)

    def scores(head, dst, n):
        dst[:, n * cols:(n + 1) * cols] = nt(qhat_ref[head], khat[pl.ds(n * cols, cols), :])

    def future_band(p):
        future = (lane >= 127 - 10) & (lane <= 126)
        for g in range(2):
            w = nt(q_ref[:, q_cols(p, g)], rev[...])
            for f in range(rows // LANES):
                sub = w[f * LANES:(f + 1) * LANES]
                near = skew(sub[:, (2 - f) * LANES:(3 - f) * LANES], 0)
                far = skew(sub[:, (1 - f) * LANES:(2 - f) * LANES], 0)
                both = jnp.where(row <= lane, near, far)
                fsc[g, pl.ds(8 + f * LANES, LANES), :] = jnp.where(future, both, 0.0)

    def stack_band():
        tiles = [None, None]
        for g in range(2):
            for a in range(qtaps):
                slot = qtaps * g + a
                part = pltpu.roll(fsc[g, pl.ds(8 - a, rows), :], (16 * slot + 16) % LANES, 1)
                i = slot // 8
                tiles[i] = part if tiles[i] is None else tiles[i] + part
        fst[:, 0:LANES] = tiles[0]
        fst[:, LANES:] = tiles[1]

    def correction(p, h, dst):
        taps = band_ref[kv * hk + p * 2 + h]
        for u in range(5, 15):
            msc[pl.ds(u, 16, stride=16), :] = pltpu.roll(taps, 21 - u, 1)
        m = msc[...]
        mhi = m.astype(BF)
        mlow = (m - mhi.astype(F32)).astype(BF)
        x = fst[...]
        xhi = x.astype(BF)
        xlow = (x - xhi.astype(F32)).astype(BF)
        wide = jnp.dot(xhi, jnp.concatenate([mhi, mlow], axis=1), preferred_element_type=F32)
        c = wide[:, :LANES] + wide[:, LANES:] + jnp.dot(xlow, mhi, preferred_element_type=F32)
        for f in range(rows // LANES):
            dst[pl.ds(f * LANES, LANES), :] = skew(c[f * LANES:(f + 1) * LANES], 112)

    def correct(s, corr):
        for f in range(rows // LANES):
            part = pl.ds(f * LANES, LANES)
            r = corr[part, :]
            for e in range(2):
                y = lane - row + (16 if e else -112)
                n = block0 - 1 + f + e
                low = jnp.where(n == -1, LANES - shift, 0)
                high = jnp.where(n == nblk - 1, LANES - shift, LANES)
                high = jnp.where((n >= -1) & (n < nblk), high, 0)
                at = jnp.where(n == -1, nblk - 1, jnp.clip(n, 0, nblk - 1))
                ok = (y >= 7) & (y <= 16) & (lane >= low) & (lane < high)
                where = (part, pl.ds(pl.multiple_of(at * LANES, LANES), LANES))
                s[where] = s[where] - jnp.where(ok, r, 0.0)

    def peak_of(masked, s, n, top):
        for m in range(n * cols // LANES, (n + 1) * cols // LANES):
            where = (slice(None), slice(m * LANES, (m + 1) * LANES))
            part = s[where]
            if masked:
                col = iota((1, LANES), 1) + (m * LANES + shift)
                if m == nblk - 1:
                    col = jnp.where(col >= keys_here, col - keys_here, col)
                part = jnp.where(col <= diag + iota((rows, 1), 0), part, NEG)
                s[where] = part
            top = part if top is None else jnp.maximum(top, part)
        return top

    def weigh(s, peak, n, acc):
        w = jnp.exp2(s[:, n * cols:(n + 1) * cols] - peak).astype(BF)
        o = jnp.dot(w, vhat[pl.ds(n * cols, cols), :], preferred_element_type=F32)
        return o if acc is None else acc + o

    def store(p, h, o, peak):
        total = o[:, LANES:]
        head = p * 2 + h
        out[:, pl.ds(pl.multiple_of(head * LANES, LANES), LANES)] = (o[:, :LANES] / total).astype(BF)
        stat[...] = jnp.where(iota((rows, LANES), 1) == head, peak + jnp.log2(total), stat[...])

    ncol = keys_here // cols

    def half_step(masked, p, h, more, ahead):
        s, corr = (sa, ca) if h == 0 else (sb, cb)
        s2 = sb if h == 0 else sa
        steps = [functools.partial(scores, 2 * p + h + 1, s2, n) for n in range(ncol)] if more else []

        def one():
            if steps:
                steps.pop(0)()

        one()
        if masked:
            correct(s, corr)
        top = None
        for n in range(ncol):
            top = peak_of(masked, s, n, top)
        peak = jnp.max(top, axis=1, keepdims=True)
        one()
        acc = None
        for n in range(ncol):
            acc = weigh(s, peak, n, acc)
            if n % 2:
                one()
        while steps:
            one()
        store(p, h, acc, peak)
        if masked and h == 0:
            correction(p, 1, cb)
            if ahead:
                future_band(p + 1)
        if masked and h == 1 and ahead:
            stack_band()
            correction(p + 1, 0, ca)

    def run(masked):
        if masked:
            win = kext[pl.ds(base + diag, nwin), :].astype(BF)
            flip = (iota((nwin, nwin), 0) + iota((nwin, nwin), 1) == nwin - 1).astype(F32).astype(BF)
            rev[...] = jnp.dot(flip, win, preferred_element_type=F32).astype(BF)
            fsc[:, 0:8, :] = jnp.zeros((2, 8, LANES), F32)
            msc[...] = jnp.zeros((2 * LANES, LANES), F32)
            future_band(0)
            stack_band()
            correction(0, 0, ca)
        for n in range(ncol):
            scores(0, sa, n)

        def body(p, c):
            half_step(masked, p, 0, True, True)
            half_step(masked, p, 1, True, True)
            return c

        if pairs > 1:
            lax.fori_loop(0, pairs - 1, body, 0)
        half_step(masked, pairs - 1, 0, True, False)
        half_step(masked, pairs - 1, 1, False, False)

    stat[...] = jnp.zeros((rows, LANES), F32)

    @pl.when(diag > keys_here + 8)
    def _():
        run(False)

    @pl.when(has_diag)
    def _():
        run(True)

    @pl.when(diag < 1 - rows)
    def _():
        out[...] = jnp.zeros_like(out)
        stat[...] = jnp.where(iota((rows, LANES), 1) < hk, NEG, 0.0)

    half = rows // 2
    side = lax.rem(seq // split_bit, 2)
    stats = pack_stats(stat[...], hk)
    stat[...] = stats
    for ref, part in ((keep_ref, side), (send_ref, 1 - side)):
        at = pl.multiple_of(part * half, half)
        ref[:, :hk * LANES] = out[pl.ds(at, half), :]
        ref[:, hk * LANES:] = stat[pl.ds(at, half), :].astype(BF)


def attend(kv, qtaps, offset, qhat, q2, k2, v2, left, right, band):
    hk, rows, depth = qhat.shape
    kvs, keys_here, _ = k2.shape
    heads = hk * kvs
    page = left.shape[0]
    ktaps = depth // LANES
    dims = (rows, heads, kvs, page, qtaps, ktaps, keys_here, 1)
    smem = pl.BlockSpec(memory_space=pltpu.SMEM)
    vmem = pl.BlockSpec(memory_space=pltpu.VMEM)
    width = hk * LANES + LANES
    shape = jax.ShapeDtypeStruct((rows // 2, width), BF)
    flops = 2 * hk * rows * keys_here * (ktaps + 2) * LANES
    return pl.pallas_call(
        functools.partial(attend_kernel, dims, kv),
        out_shape=(shape, shape),
        in_specs=[smem] + [vmem] * 7,
        out_specs=(vmem, vmem),
        scratch_shapes=[
            pltpu.VMEM((HEAD_PAD + keys_here + TAIL_PAD, LANES), F32),
            pltpu.VMEM((keys_here + 16, LANES), F32),
            pltpu.VMEM((LANES + 16, LANES), F32),
            pltpu.VMEM((keys_here + 2 * VPAD, LANES), F32),
            pltpu.VMEM((keys_here, ktaps * LANES), BF),
            pltpu.VMEM((keys_here, 2 * LANES), BF),
            pltpu.VMEM((rows, keys_here), F32),
            pltpu.VMEM((rows, keys_here), F32),
            pltpu.VMEM((rows, LANES), F32),
            pltpu.VMEM((rows, LANES), F32),
            pltpu.VMEM((rows, hk * LANES), BF),
            pltpu.VMEM((rows, LANES), F32),
            pltpu.VMEM((3 * LANES, LANES), BF),
            pltpu.VMEM((2, rows + 8, LANES), F32),
            pltpu.VMEM((rows, 2 * LANES), F32),
            pltpu.VMEM((2 * LANES, LANES), F32),
        ],
        compiler_params=pltpu.CompilerParams(vmem_limit_bytes=22 * 2**20),
        cost_estimate=pl.CostEstimate(flops=flops, bytes_accessed=4 * 2**20, transcendentals=hk * rows * keys_here),
        name=f"attend{kv}",
    )(offset, qhat, q2, k2, v2, left, right, band)


def edge_kernel(table_ref, keys_ref, first_ref, last_ref, sem):
    pages = keys_ref.shape[0]
    copies = [
        pltpu.make_async_copy(keys_ref.at[table_ref[p]], ref, sem.at[i])
        for i, (p, ref) in enumerate(((0, first_ref), (pages - 1, last_ref)))
    ]
    for c in copies:
        c.start()
    for c in copies:
        c.wait()


def edge_pages(table, keys):
    one = jax.ShapeDtypeStruct(keys.shape[1:], keys.dtype)
    vmem = pl.BlockSpec(memory_space=pltpu.VMEM)
    return pl.pallas_call(
        edge_kernel,
        out_shape=(one, one),
        in_specs=[pl.BlockSpec(memory_space=pltpu.SMEM), pl.BlockSpec(memory_space=pl.ANY)],
        out_specs=(vmem, vmem),
        scratch_shapes=[pltpu.SemaphoreType.DMA((2,))],
        compiler_params=pltpu.CompilerParams(vmem_limit_bytes=2**20),
        name="edges",
    )(table, keys)


def place_in(level):
    seq = lax.axis_index("seq")
    place = 0
    for bit in level:
        place = place * 2 + lax.rem(seq // bit, 2)
    return place


def mask_of(level, rel):
    return sum(bit for i, bit in enumerate(reversed(level)) if rel >> i & 1)


def merge_kernel(hk, came, level, *refs):
    ins, outs = refs[:came], refs[came:]
    wide = hk * LANES
    lses = [unpack_stats(r[:, wide:], hk) for r in ins]
    top = functools.reduce(jnp.maximum, lses)
    lse = top + jnp.log2(sum(jnp.exp2(x - top) for x in lses))
    weights = [jnp.exp2(x - lse) for x in lses]
    rows = ins[0].shape[0]
    target = outs[-1] if level else outs[0]
    for h in range(hk):
        cols = slice(h * LANES, (h + 1) * LANES)
        mixed = sum(r[:, cols].astype(F32) * w[:, h:h + 1] for r, w in zip(ins, weights))
        target[:, cols] = mixed.astype(target.dtype)
    if level:
        target[:, wide:] = pack_stats(jnp.where(iota((rows, LANES), 1) < hk, lse, 0.0), hk)
        parts = 1 << len(level)
        size = rows // parts
        place = place_in(level)
        for rel in range(parts):
            at = pl.multiple_of(jnp.bitwise_xor(place, rel) * size, size)
            outs[rel][...] = target[pl.ds(at, size), :].astype(BF)


def merge(parts, hk, level):
    rows, width = parts[0].shape
    vmem = pl.BlockSpec(memory_space=pltpu.VMEM)
    if level:
        count = 1 << len(level)
        shapes = (jax.ShapeDtypeStruct((rows // count, width), BF),) * count
        specs = (vmem,) * count
        scratch = [pltpu.VMEM((rows, width), F32)]
    else:
        shapes, specs, scratch = jax.ShapeDtypeStruct((rows, hk * LANES), BF), vmem, []
    return pl.pallas_call(
        functools.partial(merge_kernel, hk, len(parts), level),
        out_shape=shapes,
        in_specs=[vmem] * len(parts),
        out_specs=specs,
        scratch_shapes=scratch,
        compiler_params=pltpu.CompilerParams(vmem_limit_bytes=4 * 2**20),
        cost_estimate=pl.CostEstimate(flops=4 * rows * width, bytes_accessed=6 * rows * width, transcendentals=rows * LANES * 5),
        name=f"merge{len(parts)}",
    )(*parts)


def project_kernel(chunks, heads_axis, *refs):
    xs = refs[:-4]
    w_ref, keep_ref, send_ref, xbuf = refs[-4:]
    count = lax.axis_size("seq")
    mine = place_in([1 << i for i in range(count.bit_length() - 1)])
    rows = xbuf.shape[0]
    unit = rows // count
    per = len(xs) // chunks
    width = xs[0].shape[1]
    for c in range(chunks):
        cols = slice(c * width, (c + 1) * width)
        held = 0
        for x_ref in xs[c * per:(c + 1) * per]:
            for k in range(x_ref.shape[0] // unit):
                to = jnp.bitwise_xor(mine, held)
                xbuf[pl.ds(pl.multiple_of(to * unit, unit), unit), cols] = (
                    x_ref[pl.ds(k * unit, unit), :].astype(xbuf.dtype))
                held += 1
    y = jnp.dot(xbuf[...].astype(BF), w_ref[...], preferred_element_type=F32)
    core = lax.rem(lax.axis_index("head"), 2)
    block = rows // heads_axis
    for g in range(heads_axis // 2):
        even = y[(2 * g) * block:(2 * g + 1) * block]
        odd = y[(2 * g + 1) * block:(2 * g + 2) * block]
        keep_ref[pl.ds(g * block, block), :] = jnp.where(core == 0, even, odd)
        send_ref[pl.ds(g * block, block), :] = jnp.where(core == 0, odd, even).astype(BF)


def project(chunks, pieces, weight, rows):
    heads_axis = lax.axis_size("head")
    vmem = pl.BlockSpec(memory_space=pltpu.VMEM)
    depth, cols = weight.shape
    unit = rows // lax.axis_size("seq")
    return pl.pallas_call(
        functools.partial(project_kernel, chunks, heads_axis),
        out_shape=(jax.ShapeDtypeStruct((rows // 2, cols), F32), jax.ShapeDtypeStruct((rows // 2, cols), BF)),
        in_specs=[vmem] * (len(pieces) + 1),
        out_specs=(vmem, vmem),
        scratch_shapes=[pltpu.VMEM((rows, depth), BF if unit % 16 == 0 else F32)],
        compiler_params=pltpu.CompilerParams(vmem_limit_bytes=12 * 2**20),
        cost_estimate=pl.CostEstimate(flops=2 * rows * depth * cols, bytes_accessed=2 * depth * cols, transcendentals=0),
        name="project",
    )(*pieces, weight)


def swap(x, axis, bit):
    count = lax.axis_size(axis)
    return lax.ppermute(x, axis, [(i, i ^ bit) for i in range(count)])


def per_device(queries, keys, values, page_table, offset, conv_kernel, head_mix, out_weight):
    rows, heads, head_dim = queries.shape
    pages, page, kvs, _ = keys.shape
    hk = heads // kvs
    seq_count = lax.axis_size("seq")
    head_count = lax.axis_size("head")

    ends = seq_count - 1

    first, last = edge_pages(page_table, keys)
    left = lax.ppermute(last, "seq", [(i, i + 1) for i in range(ends)])
    right = lax.ppermute(first, "seq", [(i + 1, i) for i in range(ends)])

    q2, k2, v2, band, *qhats = prepare(
        page_table, head_mix.T, jnp.transpose(conv_kernel, (1, 2, 0)), queries, keys, values)

    bits = [1 << i for i in range(seq_count.bit_length() - 1)]
    levels = [bits[:1]] + [bits[i:i + 2] for i in range(1, len(bits), 2)]
    pieces = []
    for kv in range(kvs):
        parts = attend(kv, conv_kernel.shape[1], offset, qhats[kv], q2, k2, v2, left, right, band)
        for i, level in enumerate(levels):
            got = [swap(x, "seq", mask_of(level, rel)) for rel, x in enumerate(parts) if rel]
            parts = merge([parts[0], *got], hk, levels[i + 1] if i + 1 < len(levels) else None)
        held = [parts]
        for level in reversed(levels):
            whole = held[0] if len(held) == 1 else jnp.concatenate(held, axis=0)
            held += [swap(whole, "seq", mask_of(level, rel)) for rel in range(1, 1 << len(level))]
        pieces += held

    keep, send = project(kvs, pieces, out_weight, rows)
    me = lax.axis_index("head")
    got = swap(send, "head", 1)
    total = keep + got.astype(F32)
    block = rows // head_count
    bit = 2
    while bit < head_count:
        parts = total.reshape(-1, 2, block, total.shape[1])
        high = (me // bit) % 2 == 1
        mine = jnp.where(high, parts[:, 1], parts[:, 0])
        other = jnp.where(high, parts[:, 0], parts[:, 1]).astype(BF)
        got = swap(other, "head", bit)
        total = (mine + got.astype(F32)).reshape(-1, total.shape[1])
        bit *= 2
    return total.astype(BF)


def solution(mesh):
    placed = (
        P(None, "head", None),
        P("seq", None, "head", None),
        P("seq", None, "head", None),
        P("seq"),
        P(),
        P("head", None, None),
        P("head", None),
        P("head", "seq"),
    )
    return jax.shard_map(
        per_device, mesh=mesh, in_specs=placed, out_specs=P("head", "seq"), check_vma=False
    )
```

```python
import functools
import math

import jax
import jax.numpy as jnp
from jax import lax
from jax.experimental import pallas as pl
from jax.experimental.pallas import tpu as pltpu
from jax.sharding import PartitionSpec as P

NEG = -1e30
BF = jnp.bfloat16
F32 = jnp.float32
LANES = 128
BAND = 32
HEAD_PAD = 272
TAIL_PAD = 416
VPAD = 128
LOG2E = 1.4426950408889634


def nt(a, b, **kw):
    return lax.dot_general(a, b, (((1,), (1,)), ((), ())), preferred_element_type=F32, **kw)


def iota(shape, dim):
    return lax.broadcasted_iota(jnp.int32, shape, dim)


def skew(x, shift):
    return pltpu.roll(x, shift, 1, stride=1, stride_axis=0)


def pack_stats(lse, heads):
    hi = lse.astype(BF).astype(F32)
    mid = (lse - hi).astype(BF).astype(F32)
    low = lse - hi - mid
    return hi + pltpu.roll(mid, heads, 1) + pltpu.roll(low, 2 * heads, 1)


def unpack_stats(x, heads):
    x = x.astype(F32)
    return x + pltpu.roll(x, LANES - heads, 1) + pltpu.roll(x, LANES - 2 * heads, 1)


def prepare_kernel(dims, table_ref, mix_far, conv_far, q_far, k_far, v_far,
                   q2_ref, k2_ref, v2_ref, band_ref, *rest):
    rows, heads, kvs, pages, page, qtaps, ktaps = dims
    qhats, rest = rest[:kvs], rest[kvs:]
    (mix_ref, conv_ref, q_ref, k_ref, v_ref, sem, q32, rows_sc, base_sc, *toeps) = rest
    copies = [
        pltpu.make_async_copy(x, ref, sem.at[i])
        for i, (x, ref) in enumerate(
            zip((mix_far, conv_far, q_far, k_far, v_far), (mix_ref, conv_ref, q_ref, k_ref, v_ref)))
    ]
    for c in copies:
        c.start()
    pairs = heads // 2
    scale = LOG2E / math.sqrt(LANES)
    copies[0].wait()
    copies[1].wait()
    turned = conv_ref[...]
    conv = jnp.swapaxes(turned, 0, 1)
    lane = iota((ktaps, LANES), 1)
    lane2 = iota((qtaps, LANES), 1) + iota((qtaps, LANES), 0)
    rows_all = []
    for h in range(heads):
        rows_all.append(sum(jnp.where(lane == BAND - a, conv[a][:, h:h + 1], 0.0) for a in range(qtaps)))
        base_sc[h] = sum(jnp.where(lane2 == 15 - b, turned[b][:, h:h + 1], 0.0) for b in range(ktaps))
    band_ref[...] = jnp.zeros_like(band_ref)
    for h in range(heads):
        for g in range(2):
            src = h // 2 * 2 + g
            band_ref[h, g * qtaps:(g + 1) * qtaps, :] = base_sc[src] * (mix_ref[g:g + 1, h:h + 1] * scale)
        rows_sc[h] = rows_all[h // 2 * 2] * (mix_ref[0:1, h:h + 1] * scale) + pltpu.roll(
            rows_all[h // 2 * 2 + 1], 2 * BAND, 1) * (mix_ref[1:2, h:h + 1] * scale)

    copies[2].wait()
    q32[...] = q_ref[...].reshape(rows * heads, LANES).astype(F32)
    for h in range(heads):
        q2_ref[:, h * LANES:(h + 1) * LANES] = q32[pl.ds(h, rows, stride=heads), :].astype(BF)

    def make_queries(p, dst, head, toep):
        per = ktaps * BAND
        for h in range(2):
            for b in range(ktaps):
                t32 = skew(jnp.broadcast_to(rows_sc[2 * p + h, b:b + 1, :], (BAND, LANES)), 0)
                hi = t32.astype(BF)
                at = h * per + b * BAND
                toep[pl.ds(at, BAND), 0:LANES] = hi
                toep[pl.ds(at, BAND), LANES:] = (t32 - hi.astype(F32)).astype(BF)
        for t in range(rows // (2 * BAND)):
            r0 = t * 2 * BAND
            halves = []
            for g in range(2):
                where = pl.ds(pl.multiple_of((p * 2 + g) * LANES, LANES), LANES)
                two = q2_ref[pl.ds(r0, 2 * BAND), where]
                if t == 0:
                    one = jnp.concatenate([jnp.zeros((BAND, LANES), BF), two[:BAND]], axis=0)
                else:
                    one = q2_ref[pl.ds(r0 - BAND, 2 * BAND), where]
                halves.append(jnp.concatenate([one, two], axis=1))
            rhs = jnp.concatenate(halves + halves, axis=0)
            y = jnp.dot(toep[...], rhs, preferred_element_type=F32)
            for h in range(2):
                for b in range(ktaps):
                    for e in range(2):
                        at = h * per + b * BAND
                        dst[head + h, pl.ds(r0 + e * BAND, BAND), b * LANES:(b + 1) * LANES] = (
                            y[at:at + BAND, e * LANES:(e + 1) * LANES].astype(BF))

    for kv in range(kvs):
        each = pairs // kvs

        def body(i, c, kv=kv, each=each):
            for j, toep in enumerate(toeps):
                p = i * len(toeps) + j
                make_queries(kv * each + p, qhats[kv], 2 * p, toep)
            return c

        lax.fori_loop(0, each // len(toeps), body, 0)
    copies[3].wait()
    copies[4].wait()
    for p in range(pages):
        keys = k_ref[table_ref[p]].astype(F32)
        values = v_ref[table_ref[p]].astype(F32)
        for kv in range(kvs):
            k2_ref[kv, p * page:(p + 1) * page, :] = keys[:, kv, :]
            v2_ref[kv, p * page:(p + 1) * page, :] = values[:, kv, :]


def prepare(table, mix, conv, queries, keys, values):
    rows, heads, _ = queries.shape
    pages, page, kvs, _ = keys.shape
    ktaps, qtaps, _ = conv.shape
    smem = pl.BlockSpec(memory_space=pltpu.SMEM)
    vmem = pl.BlockSpec(memory_space=pltpu.VMEM)
    store = jax.ShapeDtypeStruct((kvs, pages * page, LANES), F32)
    toep = pltpu.VMEM((2 * ktaps * BAND, 2 * LANES), BF)
    return pl.pallas_call(
        functools.partial(prepare_kernel, (rows, heads, kvs, pages, page, qtaps, ktaps)),
        out_shape=(
            jax.ShapeDtypeStruct((rows, heads * LANES), BF),
            store,
            store,
            jax.ShapeDtypeStruct((heads, 16, LANES), F32),
        )
        + (jax.ShapeDtypeStruct((heads // kvs, rows, ktaps * LANES), BF),) * kvs,
        in_specs=[smem] + [pl.BlockSpec(memory_space=pltpu.HBM)] * 5,
        out_specs=(vmem,) * (4 + kvs),
        scratch_shapes=[
            pltpu.VMEM(mix.shape, F32),
            pltpu.VMEM(conv.shape, F32),
            pltpu.VMEM(queries.shape, BF),
            pltpu.VMEM(keys.shape, BF),
            pltpu.VMEM(values.shape, BF),
            pltpu.SemaphoreType.DMA((5,)),
            pltpu.VMEM((rows * heads, LANES), F32),
            pltpu.VMEM((heads, ktaps, LANES), F32),
            pltpu.VMEM((heads, qtaps, LANES), F32),
            toep,
            toep,
        ],
        compiler_params=pltpu.CompilerParams(vmem_limit_bytes=26 * 2**20),
        cost_estimate=pl.CostEstimate(flops=heads * rows * ktaps * LANES * 256 * 2, bytes_accessed=16 * 2**20, transcendentals=0),
        name="prepare",
    )(table, mix, conv, queries, keys, values)


def attend_kernel(dims, kv, off_ref, qhat_ref, q_ref, k_ref, v_ref, left_ref, right_ref,
                  band_ref, keep_ref, send_ref,
                  kext, krot, kwrap, vext, khat, vhat, sa, sb, ca, cb, out, stat, rev, fsc, fst, msc):
    rows, heads, kvs, page, qtaps, ktaps, keys_here, split_bit = dims
    hk = heads // kvs
    pairs = hk // 2
    rim = (ktaps - 1) // 2
    nblk = keys_here // LANES
    base = HEAD_PAD
    seq = lax.axis_index("seq")
    diag = off_ref[0] - seq * keys_here
    has_diag = (diag >= 1 - rows) & (diag <= keys_here + 8)
    shift = jnp.where(has_diag, lax.rem(diag + 2 * LANES, LANES), 0)

    kext[pl.ds(0, base - page), :] = jnp.zeros((base - page, LANES), F32)
    kext[pl.ds(base + keys_here + page, TAIL_PAD - page), :] = jnp.zeros((TAIL_PAD - page, LANES), F32)
    kext[pl.ds(base - page, page), :] = left_ref[:, kv, :].astype(F32)
    kext[pl.ds(base + keys_here, page), :] = right_ref[:, kv, :].astype(F32)
    kext[pl.ds(base, keys_here), :] = k_ref[kv]
    vext[pl.ds(0, VPAD), :] = jnp.zeros((VPAD, LANES), F32)
    vext[pl.ds(VPAD + keys_here, VPAD), :] = jnp.zeros((VPAD, LANES), F32)
    vext[pl.ds(VPAD, keys_here), :] = v_ref[kv]
    krot[...] = kext[pl.ds(base - 8 + shift, keys_here + 16), :]
    kwrap[...] = kext[pl.ds(base - 8 - LANES + shift, LANES + 16), :]
    first = iota((LANES, LANES), 0) < LANES - shift
    for n in range(nblk):
        for b in range(ktaps):
            part = krot[pl.ds(n * LANES + 8 + b - rim, LANES), :]
            if n == nblk - 1:
                part = jnp.where(first, part, kwrap[pl.ds(8 + b - rim, LANES), :])
            khat[pl.ds(n * LANES, LANES), b * LANES:(b + 1) * LANES] = part.astype(BF)
        part = vext[pl.ds(VPAD + n * LANES + shift, LANES), :]
        if n == nblk - 1:
            part = jnp.where(first, part, vext[pl.ds(shift, LANES), :])
        vhat[pl.ds(n * LANES, LANES), 0:LANES] = part.astype(BF)
    vhat[:, LANES:] = jnp.ones((keys_here, LANES), BF)

    cols = 2 * LANES
    nwin = 3 * LANES
    lane = iota((LANES, LANES), 1)
    row = iota((LANES, LANES), 0)
    block0 = (diag + 2 * LANES - shift) // LANES - 2

    def q_cols(p, g):
        return pl.ds(pl.multiple_of(((kv * pairs + p) * 2 + g) * LANES, LANES), LANES)

    def scores(head, dst, n):
        dst[:, n * cols:(n + 1) * cols] = nt(qhat_ref[head], khat[pl.ds(n * cols, cols), :])

    def future_band(p):
        future = (lane >= 127 - 10) & (lane <= 126)
        for g in range(2):
            w = nt(q_ref[:, q_cols(p, g)], rev[...])
            for f in range(rows // LANES):
                sub = w[f * LANES:(f + 1) * LANES]
                near = skew(sub[:, (2 - f) * LANES:(3 - f) * LANES], 0)
                far = skew(sub[:, (1 - f) * LANES:(2 - f) * LANES], 0)
                both = jnp.where(row <= lane, near, far)
                fsc[g, pl.ds(8 + f * LANES, LANES), :] = jnp.where(future, both, 0.0)

    def stack_band():
        tiles = [None, None]
        for g in range(2):
            for a in range(qtaps):
                slot = qtaps * g + a
                part = pltpu.roll(fsc[g, pl.ds(8 - a, rows), :], (16 * slot + 16) % LANES, 1)
                i = slot // 8
                tiles[i] = part if tiles[i] is None else tiles[i] + part
        fst[:, 0:LANES] = tiles[0]
        fst[:, LANES:] = tiles[1]

    def correction(p, h, dst):
        taps = band_ref[kv * hk + p * 2 + h]
        for u in range(5, 15):
            msc[pl.ds(u, 16, stride=16), :] = pltpu.roll(taps, 21 - u, 1)
        m = msc[...]
        mhi = m.astype(BF)
        mlow = (m - mhi.astype(F32)).astype(BF)
        x = fst[...]
        xhi = x.astype(BF)
        xlow = (x - xhi.astype(F32)).astype(BF)
        wide = jnp.dot(xhi, jnp.concatenate([mhi, mlow], axis=1), preferred_element_type=F32)
        c = wide[:, :LANES] + wide[:, LANES:] + jnp.dot(xlow, mhi, preferred_element_type=F32)
        for f in range(rows // LANES):
            dst[pl.ds(f * LANES, LANES), :] = skew(c[f * LANES:(f + 1) * LANES], 112)

    def correct(s, corr):
        for f in range(rows // LANES):
            part = pl.ds(f * LANES, LANES)
            r = corr[part, :]
            for e in range(2):
                y = lane - row + (16 if e else -112)
                n = block0 - 1 + f + e
                low = jnp.where(n == -1, LANES - shift, 0)
                high = jnp.where(n == nblk - 1, LANES - shift, LANES)
                high = jnp.where((n >= -1) & (n < nblk), high, 0)
                at = jnp.where(n == -1, nblk - 1, jnp.clip(n, 0, nblk - 1))
                ok = (y >= 7) & (y <= 16) & (lane >= low) & (lane < high)
                where = (part, pl.ds(pl.multiple_of(at * LANES, LANES), LANES))
                s[where] = s[where] - jnp.where(ok, r, 0.0)

    def peak_of(masked, s, n, top):
        for m in range(n * cols // LANES, (n + 1) * cols // LANES):
            where = (slice(None), slice(m * LANES, (m + 1) * LANES))
            part = s[where]
            if masked:
                col = iota((1, LANES), 1) + (m * LANES + shift)
                if m == nblk - 1:
                    col = jnp.where(col >= keys_here, col - keys_here, col)
                part = jnp.where(col <= diag + iota((rows, 1), 0), part, NEG)
                s[where] = part
            top = part if top is None else jnp.maximum(top, part)
        return top

    def weigh(s, peak, n, acc):
        w = jnp.exp2(s[:, n * cols:(n + 1) * cols] - peak).astype(BF)
        o = jnp.dot(w, vhat[pl.ds(n * cols, cols), :], preferred_element_type=F32)
        return o if acc is None else acc + o

    def store(p, h, o, peak):
        total = o[:, LANES:]
        head = p * 2 + h
        out[:, pl.ds(pl.multiple_of(head * LANES, LANES), LANES)] = (o[:, :LANES] / total).astype(BF)
        stat[...] = jnp.where(iota((rows, LANES), 1) == head, peak + jnp.log2(total), stat[...])

    ncol = keys_here // cols

    def half_step(masked, p, h, more, ahead):
        s, corr = (sa, ca) if h == 0 else (sb, cb)
        s2 = sb if h == 0 else sa
        steps = [functools.partial(scores, 2 * p + h + 1, s2, n) for n in range(ncol)] if more else []

        def one():
            if steps:
                steps.pop(0)()

        one()
        if masked:
            correct(s, corr)
        top = None
        for n in range(ncol):
            top = peak_of(masked, s, n, top)
        peak = jnp.max(top, axis=1, keepdims=True)
        one()
        acc = None
        for n in range(ncol):
            acc = weigh(s, peak, n, acc)
            if n % 2:
                one()
        while steps:
            one()
        store(p, h, acc, peak)
        if masked and h == 0:
            correction(p, 1, cb)
            if ahead:
                future_band(p + 1)
        if masked and h == 1 and ahead:
            stack_band()
            correction(p + 1, 0, ca)

    def run(masked):
        if masked:
            win = kext[pl.ds(base + diag, nwin), :].astype(BF)
            flip = (iota((nwin, nwin), 0) + iota((nwin, nwin), 1) == nwin - 1).astype(F32).astype(BF)
            rev[...] = jnp.dot(flip, win, preferred_element_type=F32).astype(BF)
            fsc[:, 0:8, :] = jnp.zeros((2, 8, LANES), F32)
            msc[...] = jnp.zeros((2 * LANES, LANES), F32)
            future_band(0)
            stack_band()
            correction(0, 0, ca)
        for n in range(ncol):
            scores(0, sa, n)

        def body(p, c):
            half_step(masked, p, 0, True, True)
            half_step(masked, p, 1, True, True)
            return c

        if pairs > 1:
            lax.fori_loop(0, pairs - 1, body, 0)
        half_step(masked, pairs - 1, 0, True, False)
        half_step(masked, pairs - 1, 1, False, False)

    stat[...] = jnp.zeros((rows, LANES), F32)

    @pl.when(diag > keys_here + 8)
    def _():
        run(False)

    @pl.when(has_diag)
    def _():
        run(True)

    @pl.when(diag < 1 - rows)
    def _():
        out[...] = jnp.zeros_like(out)
        stat[...] = jnp.where(iota((rows, LANES), 1) < hk, NEG, 0.0)

    half = rows // 2
    side = lax.rem(seq // split_bit, 2)
    stats = pack_stats(stat[...], hk)
    stat[...] = stats
    for ref, part in ((keep_ref, side), (send_ref, 1 - side)):
        at = pl.multiple_of(part * half, half)
        ref[:, :hk * LANES] = out[pl.ds(at, half), :]
        ref[:, hk * LANES:] = stat[pl.ds(at, half), :].astype(BF)


def attend(kv, qtaps, offset, qhat, q2, k2, v2, left, right, band):
    hk, rows, depth = qhat.shape
    kvs, keys_here, _ = k2.shape
    heads = hk * kvs
    page = left.shape[0]
    ktaps = depth // LANES
    dims = (rows, heads, kvs, page, qtaps, ktaps, keys_here, 1)
    smem = pl.BlockSpec(memory_space=pltpu.SMEM)
    vmem = pl.BlockSpec(memory_space=pltpu.VMEM)
    width = hk * LANES + LANES
    shape = jax.ShapeDtypeStruct((rows // 2, width), BF)
    flops = 2 * hk * rows * keys_here * (ktaps + 2) * LANES
    return pl.pallas_call(
        functools.partial(attend_kernel, dims, kv),
        out_shape=(shape, shape),
        in_specs=[smem] + [vmem] * 7,
        out_specs=(vmem, vmem),
        scratch_shapes=[
            pltpu.VMEM((HEAD_PAD + keys_here + TAIL_PAD, LANES), F32),
            pltpu.VMEM((keys_here + 16, LANES), F32),
            pltpu.VMEM((LANES + 16, LANES), F32),
            pltpu.VMEM((keys_here + 2 * VPAD, LANES), F32),
            pltpu.VMEM((keys_here, ktaps * LANES), BF),
            pltpu.VMEM((keys_here, 2 * LANES), BF),
            pltpu.VMEM((rows, keys_here), F32),
            pltpu.VMEM((rows, keys_here), F32),
            pltpu.VMEM((rows, LANES), F32),
            pltpu.VMEM((rows, LANES), F32),
            pltpu.VMEM((rows, hk * LANES), BF),
            pltpu.VMEM((rows, LANES), F32),
            pltpu.VMEM((3 * LANES, LANES), BF),
            pltpu.VMEM((2, rows + 8, LANES), F32),
            pltpu.VMEM((rows, 2 * LANES), F32),
            pltpu.VMEM((2 * LANES, LANES), F32),
        ],
        compiler_params=pltpu.CompilerParams(vmem_limit_bytes=22 * 2**20),
        cost_estimate=pl.CostEstimate(flops=flops, bytes_accessed=4 * 2**20, transcendentals=hk * rows * keys_here),
        name=f"attend{kv}",
    )(offset, qhat, q2, k2, v2, left, right, band)


def edge_kernel(table_ref, keys_ref, first_ref, last_ref, sem):
    pages = keys_ref.shape[0]
    copies = [
        pltpu.make_async_copy(keys_ref.at[table_ref[p]], ref, sem.at[i])
        for i, (p, ref) in enumerate(((0, first_ref), (pages - 1, last_ref)))
    ]
    for c in copies:
        c.start()
    for c in copies:
        c.wait()


def edge_pages(table, keys):
    one = jax.ShapeDtypeStruct(keys.shape[1:], keys.dtype)
    vmem = pl.BlockSpec(memory_space=pltpu.VMEM)
    return pl.pallas_call(
        edge_kernel,
        out_shape=(one, one),
        in_specs=[pl.BlockSpec(memory_space=pltpu.SMEM), pl.BlockSpec(memory_space=pltpu.HBM)],
        out_specs=(vmem, vmem),
        scratch_shapes=[pltpu.SemaphoreType.DMA((2,))],
        compiler_params=pltpu.CompilerParams(vmem_limit_bytes=2**20),
        cost_estimate=pl.CostEstimate(flops=2 * 10**10, bytes_accessed=2**20, transcendentals=0),
        name="edges",
    )(table, keys)


def place_in(level):
    seq = lax.axis_index("seq")
    place = 0
    for bit in level:
        place = place * 2 + lax.rem(seq // bit, 2)
    return place


def mask_of(level, rel):
    return sum(bit for i, bit in enumerate(reversed(level)) if rel >> i & 1)


def merge_kernel(hk, came, level, *refs):
    ins, outs = refs[:came], refs[came:]
    wide = hk * LANES
    lses = [unpack_stats(r[:, wide:], hk) for r in ins]
    top = functools.reduce(jnp.maximum, lses)
    lse = top + jnp.log2(sum(jnp.exp2(x - top) for x in lses))
    weights = [jnp.exp2(x - lse) for x in lses]
    rows = ins[0].shape[0]
    target = outs[-1] if level else outs[0]
    for h in range(hk):
        cols = slice(h * LANES, (h + 1) * LANES)
        mixed = sum(r[:, cols].astype(F32) * w[:, h:h + 1] for r, w in zip(ins, weights))
        target[:, cols] = mixed.astype(target.dtype)
    if level:
        target[:, wide:] = pack_stats(jnp.where(iota((rows, LANES), 1) < hk, lse, 0.0), hk)
        parts = 1 << len(level)
        size = rows // parts
        place = place_in(level)
        for rel in range(parts):
            at = pl.multiple_of(jnp.bitwise_xor(place, rel) * size, size)
            outs[rel][...] = target[pl.ds(at, size), :].astype(BF)


def merge(parts, hk, level):
    rows, width = parts[0].shape
    vmem = pl.BlockSpec(memory_space=pltpu.VMEM)
    if level:
        count = 1 << len(level)
        shapes = (jax.ShapeDtypeStruct((rows // count, width), BF),) * count
        specs = (vmem,) * count
        scratch = [pltpu.VMEM((rows, width), F32)]
    else:
        shapes, specs, scratch = jax.ShapeDtypeStruct((rows, hk * LANES), BF), vmem, []
    return pl.pallas_call(
        functools.partial(merge_kernel, hk, len(parts), level),
        out_shape=shapes,
        in_specs=[vmem] * len(parts),
        out_specs=specs,
        scratch_shapes=scratch,
        compiler_params=pltpu.CompilerParams(vmem_limit_bytes=4 * 2**20),
        cost_estimate=pl.CostEstimate(flops=4 * rows * width, bytes_accessed=6 * rows * width, transcendentals=rows * LANES * 5),
        name=f"merge{len(parts)}",
    )(*parts)


def project_kernel(chunks, heads_axis, *refs):
    xs = refs[:-4]
    w_ref, keep_ref, send_ref, xbuf = refs[-4:]
    count = lax.axis_size("seq")
    mine = place_in([1 << i for i in range(count.bit_length() - 1)])
    rows = xbuf.shape[0]
    unit = rows // count
    per = len(xs) // chunks
    width = xs[0].shape[1]
    for c in range(chunks):
        cols = slice(c * width, (c + 1) * width)
        held = 0
        for x_ref in xs[c * per:(c + 1) * per]:
            for k in range(x_ref.shape[0] // unit):
                to = jnp.bitwise_xor(mine, held)
                xbuf[pl.ds(pl.multiple_of(to * unit, unit), unit), cols] = (
                    x_ref[pl.ds(k * unit, unit), :].astype(xbuf.dtype))
                held += 1
    y = jnp.dot(xbuf[...].astype(BF), w_ref[...], preferred_element_type=F32)
    core = lax.rem(lax.axis_index("head"), 2)
    block = rows // heads_axis
    for g in range(heads_axis // 2):
        even = y[(2 * g) * block:(2 * g + 1) * block]
        odd = y[(2 * g + 1) * block:(2 * g + 2) * block]
        keep_ref[pl.ds(g * block, block), :] = jnp.where(core == 0, even, odd)
        send_ref[pl.ds(g * block, block), :] = jnp.where(core == 0, odd, even).astype(BF)


def project(chunks, pieces, weight, rows):
    heads_axis = lax.axis_size("head")
    vmem = pl.BlockSpec(memory_space=pltpu.VMEM)
    depth, cols = weight.shape
    unit = rows // lax.axis_size("seq")
    return pl.pallas_call(
        functools.partial(project_kernel, chunks, heads_axis),
        out_shape=(jax.ShapeDtypeStruct((rows // 2, cols), F32), jax.ShapeDtypeStruct((rows // 2, cols), BF)),
        in_specs=[vmem] * (len(pieces) + 1),
        out_specs=(vmem, vmem),
        scratch_shapes=[pltpu.VMEM((rows, depth), BF if unit % 16 == 0 else F32)],
        compiler_params=pltpu.CompilerParams(vmem_limit_bytes=12 * 2**20),
        cost_estimate=pl.CostEstimate(flops=2 * rows * depth * cols, bytes_accessed=2 * depth * cols, transcendentals=0),
        name="project",
    )(*pieces, weight)


def swap(x, axis, bit):
    count = lax.axis_size(axis)
    return lax.ppermute(x, axis, [(i, i ^ bit) for i in range(count)])


def per_device(queries, keys, values, page_table, offset, conv_kernel, head_mix, out_weight):
    rows, heads, head_dim = queries.shape
    pages, page, kvs, _ = keys.shape
    hk = heads // kvs
    seq_count = lax.axis_size("seq")
    head_count = lax.axis_size("head")

    ends = seq_count - 1

    first, last = edge_pages(page_table, keys)
    left = lax.ppermute(last, "seq", [(i, i + 1) for i in range(ends)])
    right = lax.ppermute(first, "seq", [(i + 1, i) for i in range(ends)])

    q2, k2, v2, band, *qhats = prepare(
        page_table, head_mix.T, jnp.transpose(conv_kernel, (2, 1, 0)), queries, keys, values)

    bits = [1 << i for i in range(seq_count.bit_length() - 1)]
    levels = [bits[:1]] + [bits[i:i + 2] for i in range(1, len(bits), 2)]
    pieces = []
    for kv in range(kvs):
        parts = attend(kv, conv_kernel.shape[1], offset, qhats[kv], q2, k2, v2, left, right, band)
        for i, level in enumerate(levels):
            got = [swap(x, "seq", mask_of(level, rel)) for rel, x in enumerate(parts) if rel]
            parts = merge([parts[0], *got], hk, levels[i + 1] if i + 1 < len(levels) else None)
        held = [parts]
        for level in reversed(levels):
            whole = held[0] if len(held) == 1 else jnp.concatenate(held, axis=0)
            held += [swap(whole, "seq", mask_of(level, rel)) for rel in range(1, 1 << len(level))]
        pieces += held

    keep, send = project(kvs, pieces, out_weight, rows)
    me = lax.axis_index("head")
    got = swap(send, "head", 1)
    total = keep + got.astype(F32)
    block = rows // head_count
    bit = 2
    while bit < head_count:
        parts = total.reshape(-1, 2, block, total.shape[1])
        high = (me // bit) % 2 == 1
        mine = jnp.where(high, parts[:, 1], parts[:, 0])
        other = jnp.where(high, parts[:, 0], parts[:, 1]).astype(BF)
        got = swap(other, "head", bit)
        total = (mine + got.astype(F32)).reshape(-1, total.shape[1])
        bit *= 2
    return total.astype(BF)


def solution(mesh):
    placed = (
        P(None, "head", None),
        P("seq", None, "head", None),
        P("seq", None, "head", None),
        P("seq"),
        P(),
        P("head", None, None),
        P("head", None),
        P("head", "seq"),
    )
    return jax.shard_map(
        per_device, mesh=mesh, in_specs=placed, out_specs=P("head", "seq"), check_vma=False
    )
```

```python
import functools
import math

import jax
import jax.numpy as jnp
from jax import lax
from jax.experimental import pallas as pl
from jax.experimental.pallas import tpu as pltpu
from jax.sharding import PartitionSpec as P

NEG = -1e30
BF = jnp.bfloat16
F32 = jnp.float32
LANES = 128
BAND = 32
HEAD_PAD = 272
TAIL_PAD = 416
VPAD = 128
LOG2E = 1.4426950408889634


def nt(a, b, **kw):
    return lax.dot_general(a, b, (((1,), (1,)), ((), ())), preferred_element_type=F32, **kw)


def iota(shape, dim):
    return lax.broadcasted_iota(jnp.int32, shape, dim)


def skew(x, shift):
    return pltpu.roll(x, shift, 1, stride=1, stride_axis=0)


def pack_stats(lse, heads):
    hi = lse.astype(BF).astype(F32)
    mid = (lse - hi).astype(BF).astype(F32)
    low = lse - hi - mid
    return hi + pltpu.roll(mid, heads, 1) + pltpu.roll(low, 2 * heads, 1)


def unpack_stats(x, heads):
    x = x.astype(F32)
    return x + pltpu.roll(x, LANES - heads, 1) + pltpu.roll(x, LANES - 2 * heads, 1)


def prepare_kernel(dims, table_ref, mix_ref, conv_ref, q_ref, k_ref, v_ref,
                   q2_ref, k2_ref, v2_ref, band_ref, *rest):
    rows, heads, kvs, pages, page, qtaps, ktaps = dims
    qhats, rest = rest[:kvs], rest[kvs:]
    q32, rows_sc, base_sc, *toeps = rest
    pairs = heads // 2
    scale = LOG2E / math.sqrt(LANES)
    turned = conv_ref[...]
    conv = jnp.swapaxes(turned, 0, 1)
    lane = iota((ktaps, LANES), 1)
    lane2 = iota((qtaps, LANES), 1) + iota((qtaps, LANES), 0)
    rows_all = []
    for h in range(heads):
        rows_all.append(sum(jnp.where(lane == BAND - a, conv[a][:, h:h + 1], 0.0) for a in range(qtaps)))
        base_sc[h] = sum(jnp.where(lane2 == 15 - b, turned[b][:, h:h + 1], 0.0) for b in range(ktaps))
    band_ref[...] = jnp.zeros_like(band_ref)
    for h in range(heads):
        for g in range(2):
            src = h // 2 * 2 + g
            band_ref[h, g * qtaps:(g + 1) * qtaps, :] = base_sc[src] * (mix_ref[g:g + 1, h:h + 1] * scale)
        rows_sc[h] = rows_all[h // 2 * 2] * (mix_ref[0:1, h:h + 1] * scale) + pltpu.roll(
            rows_all[h // 2 * 2 + 1], 2 * BAND, 1) * (mix_ref[1:2, h:h + 1] * scale)

    q32[...] = q_ref[...].reshape(rows * heads, LANES).astype(F32)
    for h in range(heads):
        q2_ref[:, h * LANES:(h + 1) * LANES] = q32[pl.ds(h, rows, stride=heads), :].astype(BF)

    def make_queries(p, dst, head, toep):
        per = ktaps * BAND
        for h in range(2):
            for b in range(ktaps):
                t32 = skew(jnp.broadcast_to(rows_sc[2 * p + h, b:b + 1, :], (BAND, LANES)), 0)
                hi = t32.astype(BF)
                at = h * per + b * BAND
                toep[pl.ds(at, BAND), 0:LANES] = hi
                toep[pl.ds(at, BAND), LANES:] = (t32 - hi.astype(F32)).astype(BF)
        for t in range(rows // (2 * BAND)):
            r0 = t * 2 * BAND
            halves = []
            for g in range(2):
                where = pl.ds(pl.multiple_of((p * 2 + g) * LANES, LANES), LANES)
                two = q2_ref[pl.ds(r0, 2 * BAND), where]
                if t == 0:
                    one = jnp.concatenate([jnp.zeros((BAND, LANES), BF), two[:BAND]], axis=0)
                else:
                    one = q2_ref[pl.ds(r0 - BAND, 2 * BAND), where]
                halves.append(jnp.concatenate([one, two], axis=1))
            rhs = jnp.concatenate(halves + halves, axis=0)
            y = jnp.dot(toep[...], rhs, preferred_element_type=F32)
            for h in range(2):
                for b in range(ktaps):
                    for e in range(2):
                        at = h * per + b * BAND
                        dst[head + h, pl.ds(r0 + e * BAND, BAND), b * LANES:(b + 1) * LANES] = (
                            y[at:at + BAND, e * LANES:(e + 1) * LANES].astype(BF))

    each = pairs // kvs
    share = -(-pages // pairs)
    for p in range(pairs):
        make_queries(p, qhats[p // each], 2 * (p % each), toeps[p % len(toeps)])
        for at in range(p * share, min(pages, (p + 1) * share)):
            keys = k_ref[table_ref[at]].astype(F32)
            values = v_ref[table_ref[at]].astype(F32)
            for kv in range(kvs):
                k2_ref[kv, at * page:(at + 1) * page, :] = keys[:, kv, :]
                v2_ref[kv, at * page:(at + 1) * page, :] = values[:, kv, :]


def prepare(table, mix, conv, queries, keys, values):
    rows, heads, _ = queries.shape
    pages, page, kvs, _ = keys.shape
    ktaps, qtaps, _ = conv.shape
    smem = pl.BlockSpec(memory_space=pltpu.SMEM)
    vmem = pl.BlockSpec(memory_space=pltpu.VMEM)
    store = jax.ShapeDtypeStruct((kvs, pages * page, LANES), F32)
    toep = pltpu.VMEM((2 * ktaps * BAND, 2 * LANES), BF)
    return pl.pallas_call(
        functools.partial(prepare_kernel, (rows, heads, kvs, pages, page, qtaps, ktaps)),
        out_shape=(
            jax.ShapeDtypeStruct((rows, heads * LANES), BF),
            store,
            store,
            jax.ShapeDtypeStruct((heads, 16, LANES), F32),
        )
        + (jax.ShapeDtypeStruct((heads // kvs, rows, ktaps * LANES), BF),) * kvs,
        in_specs=[smem] + [vmem] * 5,
        out_specs=(vmem,) * (4 + kvs),
        scratch_shapes=[
            pltpu.VMEM((rows * heads, LANES), F32),
            pltpu.VMEM((heads, ktaps, LANES), F32),
            pltpu.VMEM((heads, qtaps, LANES), F32),
            toep,
            toep,
            toep,
        ],
        compiler_params=pltpu.CompilerParams(vmem_limit_bytes=26 * 2**20),
        cost_estimate=pl.CostEstimate(flops=heads * rows * ktaps * LANES * 256 * 2, bytes_accessed=16 * 2**20, transcendentals=0),
        name="prepare",
    )(table, mix, conv, queries, keys, values)


def attend_kernel(dims, kv, off_ref, qhat_ref, q_ref, k_ref, v_ref, left_ref, right_ref,
                  band_ref, keep_ref, send_ref,
                  kext, krot, kwrap, vext, khat, vhat, sa, sb, ca, cb, out, stat, rev, fsc, fst, msc):
    rows, heads, kvs, page, qtaps, ktaps, keys_here, split_bit = dims
    hk = heads // kvs
    pairs = hk // 2
    rim = (ktaps - 1) // 2
    nblk = keys_here // LANES
    base = HEAD_PAD
    seq = lax.axis_index("seq")
    diag = off_ref[0] - seq * keys_here
    has_diag = (diag >= 1 - rows) & (diag <= keys_here + 8)
    shift = jnp.where(has_diag, lax.rem(diag + 2 * LANES, LANES), 0)

    kext[pl.ds(0, base - page), :] = jnp.zeros((base - page, LANES), F32)
    kext[pl.ds(base + keys_here + page, TAIL_PAD - page), :] = jnp.zeros((TAIL_PAD - page, LANES), F32)
    kext[pl.ds(base - page, page), :] = left_ref[:, kv, :].astype(F32)
    kext[pl.ds(base + keys_here, page), :] = right_ref[:, kv, :].astype(F32)
    kext[pl.ds(base, keys_here), :] = k_ref[kv]
    vext[pl.ds(0, VPAD), :] = jnp.zeros((VPAD, LANES), F32)
    vext[pl.ds(VPAD + keys_here, VPAD), :] = jnp.zeros((VPAD, LANES), F32)
    vext[pl.ds(VPAD, keys_here), :] = v_ref[kv]
    krot[...] = kext[pl.ds(base - 8 + shift, keys_here + 16), :]
    kwrap[...] = kext[pl.ds(base - 8 - LANES + shift, LANES + 16), :]
    first = iota((LANES, LANES), 0) < LANES - shift
    for n in range(nblk):
        for b in range(ktaps):
            part = krot[pl.ds(n * LANES + 8 + b - rim, LANES), :]
            if n == nblk - 1:
                part = jnp.where(first, part, kwrap[pl.ds(8 + b - rim, LANES), :])
            khat[pl.ds(n * LANES, LANES), b * LANES:(b + 1) * LANES] = part.astype(BF)
        part = vext[pl.ds(VPAD + n * LANES + shift, LANES), :]
        if n == nblk - 1:
            part = jnp.where(first, part, vext[pl.ds(shift, LANES), :])
        vhat[pl.ds(n * LANES, LANES), 0:LANES] = part.astype(BF)
    vhat[:, LANES:] = jnp.ones((keys_here, LANES), BF)

    cols = 2 * LANES
    nwin = 3 * LANES
    lane = iota((LANES, LANES), 1)
    row = iota((LANES, LANES), 0)
    block0 = (diag + 2 * LANES - shift) // LANES - 2

    def q_cols(p, g):
        return pl.ds(pl.multiple_of(((kv * pairs + p) * 2 + g) * LANES, LANES), LANES)

    def scores(head, dst, n):
        dst[:, n * cols:(n + 1) * cols] = nt(qhat_ref[head], khat[pl.ds(n * cols, cols), :])

    def future_band(p):
        future = (lane >= 127 - 10) & (lane <= 126)
        for g in range(2):
            w = nt(q_ref[:, q_cols(p, g)], rev[...])
            for f in range(rows // LANES):
                sub = w[f * LANES:(f + 1) * LANES]
                near = skew(sub[:, (2 - f) * LANES:(3 - f) * LANES], 0)
                far = skew(sub[:, (1 - f) * LANES:(2 - f) * LANES], 0)
                both = jnp.where(row <= lane, near, far)
                fsc[g, pl.ds(8 + f * LANES, LANES), :] = jnp.where(future, both, 0.0)

    def stack_band():
        tiles = [None, None]
        for g in range(2):
            for a in range(qtaps):
                slot = qtaps * g + a
                part = pltpu.roll(fsc[g, pl.ds(8 - a, rows), :], (16 * slot + 16) % LANES, 1)
                i = slot // 8
                tiles[i] = part if tiles[i] is None else tiles[i] + part
        fst[:, 0:LANES] = tiles[0]
        fst[:, LANES:] = tiles[1]

    def correction(p, h, dst):
        taps = band_ref[kv * hk + p * 2 + h]
        for u in range(5, 15):
            msc[pl.ds(u, 16, stride=16), :] = pltpu.roll(taps, 21 - u, 1)
        m = msc[...]
        mhi = m.astype(BF)
        mlow = (m - mhi.astype(F32)).astype(BF)
        x = fst[...]
        xhi = x.astype(BF)
        xlow = (x - xhi.astype(F32)).astype(BF)
        wide = jnp.dot(xhi, jnp.concatenate([mhi, mlow], axis=1), preferred_element_type=F32)
        c = wide[:, :LANES] + wide[:, LANES:] + jnp.dot(xlow, mhi, preferred_element_type=F32)
        for f in range(rows // LANES):
            dst[pl.ds(f * LANES, LANES), :] = skew(c[f * LANES:(f + 1) * LANES], 112)

    def correct(s, corr):
        for f in range(rows // LANES):
            part = pl.ds(f * LANES, LANES)
            r = corr[part, :]
            for e in range(2):
                y = lane - row + (16 if e else -112)
                n = block0 - 1 + f + e
                low = jnp.where(n == -1, LANES - shift, 0)
                high = jnp.where(n == nblk - 1, LANES - shift, LANES)
                high = jnp.where((n >= -1) & (n < nblk), high, 0)
                at = jnp.where(n == -1, nblk - 1, jnp.clip(n, 0, nblk - 1))
                ok = (y >= 7) & (y <= 16) & (lane >= low) & (lane < high)
                where = (part, pl.ds(pl.multiple_of(at * LANES, LANES), LANES))
                s[where] = s[where] - jnp.where(ok, r, 0.0)

    def masked_part(masked, s, m):
        part = s[:, m * LANES:(m + 1) * LANES]
        if not masked:
            return part
        col = iota((1, LANES), 1) + (m * LANES + shift)
        if m == nblk - 1:
            col = jnp.where(col >= keys_here, col - keys_here, col)
        return jnp.where(col <= diag + iota((rows, 1), 0), part, NEG)

    def peak_of(masked, s, n, top):
        for m in range(n * cols // LANES, (n + 1) * cols // LANES):
            part = masked_part(masked, s, m)
            top = part if top is None else jnp.maximum(top, part)
        return top

    def weigh(masked, s, peak, n, acc):
        parts = [
            jnp.exp2(masked_part(masked, s, m) - peak).astype(BF)
            for m in range(n * cols // LANES, (n + 1) * cols // LANES)
        ]
        w = jnp.concatenate(parts, axis=1)
        o = jnp.dot(w, vhat[pl.ds(n * cols, cols), :], preferred_element_type=F32)
        return o if acc is None else acc + o

    def store(p, h, o, peak):
        total = o[:, LANES:]
        head = p * 2 + h
        out[:, pl.ds(pl.multiple_of(head * LANES, LANES), LANES)] = (o[:, :LANES] / total).astype(BF)
        stat[...] = jnp.where(iota((rows, LANES), 1) == head, peak + jnp.log2(total), stat[...])

    ncol = keys_here // cols

    def half_step(masked, p, h, more, ahead):
        s, corr = (sa, ca) if h == 0 else (sb, cb)
        s2 = sb if h == 0 else sa
        steps = [functools.partial(scores, 2 * p + h + 1, s2, n) for n in range(ncol)] if more else []

        def one():
            if steps:
                steps.pop(0)()

        one()
        if masked:
            correct(s, corr)
        top = None
        for n in range(ncol):
            top = peak_of(masked, s, n, top)
        peak = jnp.max(top, axis=1, keepdims=True)
        one()
        acc = None
        for n in range(ncol):
            acc = weigh(masked, s, peak, n, acc)
            if n % 2:
                one()
        while steps:
            one()
        store(p, h, acc, peak)
        if masked and h == 0:
            correction(p, 1, cb)
            if ahead:
                future_band(p + 1)
        if masked and h == 1 and ahead:
            stack_band()
            correction(p + 1, 0, ca)

    def run(masked):
        if masked:
            win = kext[pl.ds(base + diag, nwin), :].astype(BF)
            flip = (iota((nwin, nwin), 0) + iota((nwin, nwin), 1) == nwin - 1).astype(F32).astype(BF)
            rev[...] = jnp.dot(flip, win, preferred_element_type=F32).astype(BF)
            fsc[:, 0:8, :] = jnp.zeros((2, 8, LANES), F32)
            msc[...] = jnp.zeros((2 * LANES, LANES), F32)
            future_band(0)
            stack_band()
            correction(0, 0, ca)
        for n in range(ncol):
            scores(0, sa, n)

        def body(p, c):
            half_step(masked, p, 0, True, True)
            half_step(masked, p, 1, True, True)
            return c

        if pairs > 1:
            lax.fori_loop(0, pairs - 1, body, 0)
        half_step(masked, pairs - 1, 0, True, False)
        half_step(masked, pairs - 1, 1, False, False)

    stat[...] = jnp.zeros((rows, LANES), F32)

    @pl.when(diag > keys_here + 8)
    def _():
        run(False)

    @pl.when(has_diag)
    def _():
        run(True)

    @pl.when(diag < 1 - rows)
    def _():
        out[...] = jnp.zeros_like(out)
        stat[...] = jnp.where(iota((rows, LANES), 1) < hk, NEG, 0.0)

    half = rows // 2
    side = lax.rem(seq // split_bit, 2)
    stats = pack_stats(stat[...], hk)
    stat[...] = stats
    for ref, part in ((keep_ref, side), (send_ref, 1 - side)):
        at = pl.multiple_of(part * half, half)
        ref[:, :hk * LANES] = out[pl.ds(at, half), :]
        ref[:, hk * LANES:] = stat[pl.ds(at, half), :].astype(BF)


def attend(kv, qtaps, offset, qhat, q2, k2, v2, left, right, band):
    hk, rows, depth = qhat.shape
    kvs, keys_here, _ = k2.shape
    heads = hk * kvs
    page = left.shape[0]
    ktaps = depth // LANES
    dims = (rows, heads, kvs, page, qtaps, ktaps, keys_here, 1)
    smem = pl.BlockSpec(memory_space=pltpu.SMEM)
    vmem = pl.BlockSpec(memory_space=pltpu.VMEM)
    width = hk * LANES + LANES
    shape = jax.ShapeDtypeStruct((rows // 2, width), BF)
    flops = 2 * hk * rows * keys_here * (ktaps + 2) * LANES
    return pl.pallas_call(
        functools.partial(attend_kernel, dims, kv),
        out_shape=(shape, shape),
        in_specs=[smem] + [vmem] * 7,
        out_specs=(vmem, vmem),
        scratch_shapes=[
            pltpu.VMEM((HEAD_PAD + keys_here + TAIL_PAD, LANES), F32),
            pltpu.VMEM((keys_here + 16, LANES), F32),
            pltpu.VMEM((LANES + 16, LANES), F32),
            pltpu.VMEM((keys_here + 2 * VPAD, LANES), F32),
            pltpu.VMEM((keys_here, ktaps * LANES), BF),
            pltpu.VMEM((keys_here, 2 * LANES), BF),
            pltpu.VMEM((rows, keys_here), F32),
            pltpu.VMEM((rows, keys_here), F32),
            pltpu.VMEM((rows, LANES), F32),
            pltpu.VMEM((rows, LANES), F32),
            pltpu.VMEM((rows, hk * LANES), BF),
            pltpu.VMEM((rows, LANES), F32),
            pltpu.VMEM((3 * LANES, LANES), BF),
            pltpu.VMEM((2, rows + 8, LANES), F32),
            pltpu.VMEM((rows, 2 * LANES), F32),
            pltpu.VMEM((2 * LANES, LANES), F32),
        ],
        compiler_params=pltpu.CompilerParams(vmem_limit_bytes=22 * 2**20),
        cost_estimate=pl.CostEstimate(flops=flops, bytes_accessed=4 * 2**20, transcendentals=hk * rows * keys_here),
        name=f"attend{kv}",
    )(offset, qhat, q2, k2, v2, left, right, band)


def edge_kernel(table_ref, keys_ref, first_ref, last_ref, sem):
    pages = keys_ref.shape[0]
    copies = [
        pltpu.make_async_copy(keys_ref.at[table_ref[p]], ref, sem.at[i])
        for i, (p, ref) in enumerate(((0, first_ref), (pages - 1, last_ref)))
    ]
    for c in copies:
        c.start()
    for c in copies:
        c.wait()


def edge_pages(table, keys):
    one = jax.ShapeDtypeStruct(keys.shape[1:], keys.dtype)
    vmem = pl.BlockSpec(memory_space=pltpu.VMEM)
    return pl.pallas_call(
        edge_kernel,
        out_shape=(one, one),
        in_specs=[pl.BlockSpec(memory_space=pltpu.SMEM), pl.BlockSpec(memory_space=pltpu.HBM)],
        out_specs=(vmem, vmem),
        scratch_shapes=[pltpu.SemaphoreType.DMA((2,))],
        compiler_params=pltpu.CompilerParams(vmem_limit_bytes=2**20),
        cost_estimate=pl.CostEstimate(flops=2 * 10**10, bytes_accessed=2**20, transcendentals=0),
        name="edges",
    )(table, keys)


def place_in(level):
    seq = lax.axis_index("seq")
    place = 0
    for bit in level:
        place = place * 2 + lax.rem(seq // bit, 2)
    return place


def mask_of(level, rel):
    return sum(bit for i, bit in enumerate(reversed(level)) if rel >> i & 1)


def merge_kernel(hk, came, level, *refs):
    ins, outs = refs[:came], refs[came:]
    wide = hk * LANES
    lses = [unpack_stats(r[:, wide:], hk) for r in ins]
    top = functools.reduce(jnp.maximum, lses)
    lse = top + jnp.log2(sum(jnp.exp2(x - top) for x in lses))
    weights = [jnp.exp2(x - lse) for x in lses]
    rows = ins[0].shape[0]
    target = outs[-1] if level else outs[0]
    for h in range(hk):
        cols = slice(h * LANES, (h + 1) * LANES)
        mixed = sum(r[:, cols].astype(F32) * w[:, h:h + 1] for r, w in zip(ins, weights))
        target[:, cols] = mixed.astype(target.dtype)
    if level:
        target[:, wide:] = pack_stats(jnp.where(iota((rows, LANES), 1) < hk, lse, 0.0), hk)
        parts = 1 << len(level)
        size = rows // parts
        place = place_in(level)
        for rel in range(parts):
            at = pl.multiple_of(jnp.bitwise_xor(place, rel) * size, size)
            outs[rel][...] = target[pl.ds(at, size), :].astype(BF)


def merge(parts, hk, level):
    rows, width = parts[0].shape
    vmem = pl.BlockSpec(memory_space=pltpu.VMEM)
    if level:
        count = 1 << len(level)
        shapes = (jax.ShapeDtypeStruct((rows // count, width), BF),) * count
        specs = (vmem,) * count
        scratch = [pltpu.VMEM((rows, width), F32)]
    else:
        shapes, specs, scratch = jax.ShapeDtypeStruct((rows, hk * LANES), BF), vmem, []
    return pl.pallas_call(
        functools.partial(merge_kernel, hk, len(parts), level),
        out_shape=shapes,
        in_specs=[vmem] * len(parts),
        out_specs=specs,
        scratch_shapes=scratch,
        compiler_params=pltpu.CompilerParams(vmem_limit_bytes=4 * 2**20),
        cost_estimate=pl.CostEstimate(flops=4 * rows * width, bytes_accessed=6 * rows * width, transcendentals=rows * LANES * 5),
        name=f"merge{len(parts)}",
    )(*parts)


def project_kernel(chunks, heads_axis, *refs):
    xs = refs[:-4]
    w_ref, keep_ref, send_ref, xbuf = refs[-4:]
    count = lax.axis_size("seq")
    mine = place_in([1 << i for i in range(count.bit_length() - 1)])
    rows = xbuf.shape[0]
    unit = rows // count
    per = len(xs) // chunks
    width = xs[0].shape[1]
    for c in range(chunks):
        cols = slice(c * width, (c + 1) * width)
        held = 0
        for x_ref in xs[c * per:(c + 1) * per]:
            for k in range(x_ref.shape[0] // unit):
                to = jnp.bitwise_xor(mine, held)
                xbuf[pl.ds(pl.multiple_of(to * unit, unit), unit), cols] = (
                    x_ref[pl.ds(k * unit, unit), :].astype(xbuf.dtype))
                held += 1
    y = jnp.dot(xbuf[...].astype(BF), w_ref[...], preferred_element_type=F32)
    core = lax.rem(lax.axis_index("head"), 2)
    block = rows // heads_axis
    for g in range(heads_axis // 2):
        even = y[(2 * g) * block:(2 * g + 1) * block]
        odd = y[(2 * g + 1) * block:(2 * g + 2) * block]
        keep_ref[pl.ds(g * block, block), :] = jnp.where(core == 0, even, odd)
        send_ref[pl.ds(g * block, block), :] = jnp.where(core == 0, odd, even).astype(BF)


def project(chunks, pieces, weight, rows):
    heads_axis = lax.axis_size("head")
    vmem = pl.BlockSpec(memory_space=pltpu.VMEM)
    depth, cols = weight.shape
    unit = rows // lax.axis_size("seq")
    return pl.pallas_call(
        functools.partial(project_kernel, chunks, heads_axis),
        out_shape=(jax.ShapeDtypeStruct((rows // 2, cols), F32), jax.ShapeDtypeStruct((rows // 2, cols), BF)),
        in_specs=[vmem] * (len(pieces) + 1),
        out_specs=(vmem, vmem),
        scratch_shapes=[pltpu.VMEM((rows, depth), BF if unit % 16 == 0 else F32)],
        compiler_params=pltpu.CompilerParams(vmem_limit_bytes=12 * 2**20),
        cost_estimate=pl.CostEstimate(flops=2 * rows * depth * cols, bytes_accessed=2 * depth * cols, transcendentals=0),
        name="project",
    )(*pieces, weight)


def swap(x, axis, bit):
    count = lax.axis_size(axis)
    return lax.ppermute(x, axis, [(i, i ^ bit) for i in range(count)])


def per_device(queries, keys, values, page_table, offset, conv_kernel, head_mix, out_weight):
    rows, heads, head_dim = queries.shape
    pages, page, kvs, _ = keys.shape
    hk = heads // kvs
    seq_count = lax.axis_size("seq")
    head_count = lax.axis_size("head")

    ends = seq_count - 1

    first, last = edge_pages(page_table, keys)
    left = lax.ppermute(last, "seq", [(i, i + 1) for i in range(ends)])
    right = lax.ppermute(first, "seq", [(i + 1, i) for i in range(ends)])

    q2, k2, v2, band, *qhats = prepare(
        page_table, head_mix.T, jnp.transpose(conv_kernel, (2, 1, 0)), queries, keys, values)

    bits = [1 << i for i in range(seq_count.bit_length() - 1)]
    levels = [bits[:1]] + [bits[i:i + 2] for i in range(1, len(bits), 2)]
    pieces = []
    for kv in range(kvs):
        parts = attend(kv, conv_kernel.shape[1], offset, qhats[kv], q2, k2, v2, left, right, band)
        for i, level in enumerate(levels):
            got = [swap(x, "seq", mask_of(level, rel)) for rel, x in enumerate(parts) if rel]
            parts = merge([parts[0], *got], hk, levels[i + 1] if i + 1 < len(levels) else None)
        held = [parts]
        for level in reversed(levels):
            whole = held[0] if len(held) == 1 else jnp.concatenate(held, axis=0)
            held += [swap(whole, "seq", mask_of(level, rel)) for rel in range(1, 1 << len(level))]
        pieces += held

    keep, send = project(kvs, pieces, out_weight, rows)
    me = lax.axis_index("head")
    got = swap(send, "head", 1)
    total = keep + got.astype(F32)
    block = rows // head_count
    bit = 2
    while bit < head_count:
        parts = total.reshape(-1, 2, block, total.shape[1])
        high = (me // bit) % 2 == 1
        mine = jnp.where(high, parts[:, 1], parts[:, 0])
        other = jnp.where(high, parts[:, 0], parts[:, 1]).astype(BF)
        got = swap(other, "head", bit)
        total = (mine + got.astype(F32)).reshape(-1, total.shape[1])
        bit *= 2
    return total.astype(BF)


def solution(mesh):
    placed = (
        P(None, "head", None),
        P("seq", None, "head", None),
        P("seq", None, "head", None),
        P("seq"),
        P(),
        P("head", None, None),
        P("head", None),
        P("head", "seq"),
    )
    return jax.shard_map(
        per_device, mesh=mesh, in_specs=placed, out_specs=P("head", "seq"), check_vma=False
    )
```

```python
import functools
import math

import jax
import jax.numpy as jnp
from jax import lax
from jax.experimental import pallas as pl
from jax.experimental.pallas import tpu as pltpu
from jax.sharding import PartitionSpec as P

NEG = -1e30
BF = jnp.bfloat16
F32 = jnp.float32
LANES = 128
BAND = 32
HEAD_PAD = 272
TAIL_PAD = 416
VPAD = 128
LOG2E = 1.4426950408889634


def nt(a, b, **kw):
    return lax.dot_general(a, b, (((1,), (1,)), ((), ())), preferred_element_type=F32, **kw)


def iota(shape, dim):
    return lax.broadcasted_iota(jnp.int32, shape, dim)


def skew(x, shift):
    return pltpu.roll(x, shift, 1, stride=1, stride_axis=0)


def pack_stats(lse, heads):
    hi = lse.astype(BF).astype(F32)
    mid = (lse - hi).astype(BF).astype(F32)
    low = lse - hi - mid
    return hi + pltpu.roll(mid, heads, 1) + pltpu.roll(low, 2 * heads, 1)


def unpack_stats(x, heads):
    x = x.astype(F32)
    return x + pltpu.roll(x, LANES - heads, 1) + pltpu.roll(x, LANES - 2 * heads, 1)


def prepare_kernel(dims, table_ref, mix_ref, conv_ref, q_ref, k_ref, v_ref,
                   q2_ref, k2_ref, v2_ref, band_ref, *rest):
    rows, heads, kvs, pages, page, qtaps, ktaps = dims
    qhats, rest = rest[:kvs], rest[kvs:]
    q32, rows_sc, base_sc, *toeps = rest
    pairs = heads // 2
    scale = LOG2E / math.sqrt(LANES)
    turned = conv_ref[...]
    conv = jnp.swapaxes(turned, 0, 1)
    lane = iota((ktaps, LANES), 1)
    lane2 = iota((qtaps, LANES), 1) + iota((qtaps, LANES), 0)
    rows_all = []
    for h in range(heads):
        rows_all.append(sum(jnp.where(lane == BAND - a, conv[a][:, h:h + 1], 0.0) for a in range(qtaps)))
        base_sc[h] = sum(jnp.where(lane2 == 15 - b, turned[b][:, h:h + 1], 0.0) for b in range(ktaps))
    band_ref[...] = jnp.zeros_like(band_ref)
    for h in range(heads):
        for g in range(2):
            src = h // 2 * 2 + g
            band_ref[h, g * qtaps:(g + 1) * qtaps, :] = base_sc[src] * (mix_ref[g:g + 1, h:h + 1] * scale)
        rows_sc[h] = rows_all[h // 2 * 2] * (mix_ref[0:1, h:h + 1] * scale) + pltpu.roll(
            rows_all[h // 2 * 2 + 1], 2 * BAND, 1) * (mix_ref[1:2, h:h + 1] * scale)

    q32[...] = q_ref[...].reshape(rows * heads, LANES).astype(F32)
    for h in range(heads):
        q2_ref[:, h * LANES:(h + 1) * LANES] = q32[pl.ds(h, rows, stride=heads), :].astype(BF)

    def make_queries(p, dst, head, toep):
        per = ktaps * BAND
        for h in range(2):
            for b in range(ktaps):
                t32 = skew(jnp.broadcast_to(rows_sc[2 * p + h, b:b + 1, :], (BAND, LANES)), 0)
                hi = t32.astype(BF)
                at = h * per + b * BAND
                toep[pl.ds(at, BAND), 0:LANES] = hi
                toep[pl.ds(at, BAND), LANES:] = (t32 - hi.astype(F32)).astype(BF)
        for t in range(rows // (2 * BAND)):
            r0 = t * 2 * BAND
            halves = []
            for g in range(2):
                where = pl.ds(pl.multiple_of((p * 2 + g) * LANES, LANES), LANES)
                two = q2_ref[pl.ds(r0, 2 * BAND), where]
                if t == 0:
                    one = jnp.concatenate([jnp.zeros((BAND, LANES), BF), two[:BAND]], axis=0)
                else:
                    one = q2_ref[pl.ds(r0 - BAND, 2 * BAND), where]
                halves.append(jnp.concatenate([one, two], axis=1))
            rhs = jnp.concatenate(halves + halves, axis=0)
            y = jnp.dot(toep[...], rhs, preferred_element_type=F32)
            for h in range(2):
                for b in range(ktaps):
                    for e in range(2):
                        at = h * per + b * BAND
                        dst[head + h, pl.ds(r0 + e * BAND, BAND), b * LANES:(b + 1) * LANES] = (
                            y[at:at + BAND, e * LANES:(e + 1) * LANES].astype(BF))

    each = pairs // kvs
    share = -(-pages // pairs)
    for p in range(pairs):
        make_queries(p, qhats[p // each], 2 * (p % each), toeps[p % len(toeps)])
        for at in range(p * share, min(pages, (p + 1) * share)):
            keys = k_ref[table_ref[at]].astype(F32)
            values = v_ref[table_ref[at]].astype(F32)
            for kv in range(kvs):
                k2_ref[kv, at * page:(at + 1) * page, :] = keys[:, kv, :]
                v2_ref[kv, at * page:(at + 1) * page, :] = values[:, kv, :]


def prepare(table, mix, conv, queries, keys, values):
    rows, heads, _ = queries.shape
    pages, page, kvs, _ = keys.shape
    ktaps, qtaps, _ = conv.shape
    smem = pl.BlockSpec(memory_space=pltpu.SMEM)
    vmem = pl.BlockSpec(memory_space=pltpu.VMEM)
    store = jax.ShapeDtypeStruct((kvs, pages * page, LANES), F32)
    toep = pltpu.VMEM((2 * ktaps * BAND, 2 * LANES), BF)
    return pl.pallas_call(
        functools.partial(prepare_kernel, (rows, heads, kvs, pages, page, qtaps, ktaps)),
        out_shape=(
            jax.ShapeDtypeStruct((rows, heads * LANES), BF),
            store,
            store,
            jax.ShapeDtypeStruct((heads, 16, LANES), F32),
        )
        + (jax.ShapeDtypeStruct((heads // kvs, rows, ktaps * LANES), BF),) * kvs,
        in_specs=[smem] + [vmem] * 5,
        out_specs=(vmem,) * (4 + kvs),
        scratch_shapes=[
            pltpu.VMEM((rows * heads, LANES), F32),
            pltpu.VMEM((heads, ktaps, LANES), F32),
            pltpu.VMEM((heads, qtaps, LANES), F32),
            toep,
            toep,
            toep,
        ],
        compiler_params=pltpu.CompilerParams(vmem_limit_bytes=26 * 2**20),
        cost_estimate=pl.CostEstimate(flops=heads * rows * ktaps * LANES * 256 * 2, bytes_accessed=16 * 2**20, transcendentals=0),
        name="prepare",
    )(table, mix, conv, queries, keys, values)


def attend_kernel(dims, kv, off_ref, qhat_ref, q_ref, k_ref, v_ref, pair_ref, next_ref,
                  band_ref, keep_ref, send_ref,
                  kext, krot, kwrap, vext, khat, vhat, sa, sb, ca, cb, out, stat, rev, fsc, fst, msc):
    rows, heads, kvs, page, qtaps, ktaps, keys_here, split_bit = dims
    hk = heads // kvs
    pairs = hk // 2
    rim = (ktaps - 1) // 2
    nblk = keys_here // LANES
    base = HEAD_PAD
    seq = lax.axis_index("seq")
    diag = off_ref[0] - seq * keys_here
    has_diag = (diag >= 1 - rows) & (diag <= keys_here + 8)
    shift = jnp.where(has_diag, lax.rem(diag + 2 * LANES, LANES), 0)

    kext[pl.ds(0, base - page), :] = jnp.zeros((base - page, LANES), F32)
    kext[pl.ds(base + keys_here + page, TAIL_PAD - page), :] = jnp.zeros((TAIL_PAD - page, LANES), F32)
    odd = lax.rem(seq, 2)
    kext[pl.ds(base - page + (1 - odd) * (keys_here + page), page), :] = pair_ref[:, kv, :].astype(F32)
    kext[pl.ds(base - page + odd * (keys_here + page), page), :] = next_ref[:, kv, :].astype(F32)
    kext[pl.ds(base, keys_here), :] = k_ref[kv]
    vext[pl.ds(0, VPAD), :] = jnp.zeros((VPAD, LANES), F32)
    vext[pl.ds(VPAD + keys_here, VPAD), :] = jnp.zeros((VPAD, LANES), F32)
    vext[pl.ds(VPAD, keys_here), :] = v_ref[kv]
    krot[...] = kext[pl.ds(base - 8 + shift, keys_here + 16), :]
    kwrap[...] = kext[pl.ds(base - 8 - LANES + shift, LANES + 16), :]
    first = iota((LANES, LANES), 0) < LANES - shift
    for n in range(nblk):
        for b in range(ktaps):
            part = krot[pl.ds(n * LANES + 8 + b - rim, LANES), :]
            if n == nblk - 1:
                part = jnp.where(first, part, kwrap[pl.ds(8 + b - rim, LANES), :])
            khat[pl.ds(n * LANES, LANES), b * LANES:(b + 1) * LANES] = part.astype(BF)
        part = vext[pl.ds(VPAD + n * LANES + shift, LANES), :]
        if n == nblk - 1:
            part = jnp.where(first, part, vext[pl.ds(shift, LANES), :])
        vhat[pl.ds(n * LANES, LANES), 0:LANES] = part.astype(BF)
    vhat[:, LANES:] = jnp.ones((keys_here, LANES), BF)

    cols = 2 * LANES
    nwin = 3 * LANES
    lane = iota((LANES, LANES), 1)
    row = iota((LANES, LANES), 0)
    block0 = (diag + 2 * LANES - shift) // LANES - 2

    def q_cols(p, g):
        return pl.ds(pl.multiple_of(((kv * pairs + p) * 2 + g) * LANES, LANES), LANES)

    def scores(head, dst, n):
        dst[:, n * cols:(n + 1) * cols] = nt(qhat_ref[head], khat[pl.ds(n * cols, cols), :])

    def future_band(p):
        future = (lane >= 127 - 10) & (lane <= 126)
        for g in range(2):
            w = nt(q_ref[:, q_cols(p, g)], rev[...])
            for f in range(rows // LANES):
                sub = w[f * LANES:(f + 1) * LANES]
                near = skew(sub[:, (2 - f) * LANES:(3 - f) * LANES], 0)
                far = skew(sub[:, (1 - f) * LANES:(2 - f) * LANES], 0)
                both = jnp.where(row <= lane, near, far)
                fsc[g, pl.ds(8 + f * LANES, LANES), :] = jnp.where(future, both, 0.0)

    def stack_band():
        tiles = [None, None]
        for g in range(2):
            for a in range(qtaps):
                slot = qtaps * g + a
                part = pltpu.roll(fsc[g, pl.ds(8 - a, rows), :], (16 * slot + 16) % LANES, 1)
                i = slot // 8
                tiles[i] = part if tiles[i] is None else tiles[i] + part
        fst[:, 0:LANES] = tiles[0]
        fst[:, LANES:] = tiles[1]

    def correction(p, h, dst):
        taps = band_ref[kv * hk + p * 2 + h]
        for u in range(5, 15):
            msc[pl.ds(u, 16, stride=16), :] = pltpu.roll(taps, 21 - u, 1)
        m = msc[...]
        mhi = m.astype(BF)
        mlow = (m - mhi.astype(F32)).astype(BF)
        x = fst[...]
        xhi = x.astype(BF)
        xlow = (x - xhi.astype(F32)).astype(BF)
        wide = jnp.dot(xhi, jnp.concatenate([mhi, mlow], axis=1), preferred_element_type=F32)
        c = wide[:, :LANES] + wide[:, LANES:] + jnp.dot(xlow, mhi, preferred_element_type=F32)
        for f in range(rows // LANES):
            dst[pl.ds(f * LANES, LANES), :] = skew(c[f * LANES:(f + 1) * LANES], 112)

    def correct(s, corr):
        for f in range(rows // LANES):
            part = pl.ds(f * LANES, LANES)
            r = corr[part, :]
            for e in range(2):
                y = lane - row + (16 if e else -112)
                n = block0 - 1 + f + e
                low = jnp.where(n == -1, LANES - shift, 0)
                high = jnp.where(n == nblk - 1, LANES - shift, LANES)
                high = jnp.where((n >= -1) & (n < nblk), high, 0)
                at = jnp.where(n == -1, nblk - 1, jnp.clip(n, 0, nblk - 1))
                ok = (y >= 7) & (y <= 16) & (lane >= low) & (lane < high)
                where = (part, pl.ds(pl.multiple_of(at * LANES, LANES), LANES))
                s[where] = s[where] - jnp.where(ok, r, 0.0)

    def masked_part(masked, s, m):
        part = s[:, m * LANES:(m + 1) * LANES]
        if not masked:
            return part
        col = iota((1, LANES), 1) + (m * LANES + shift)
        if m == nblk - 1:
            col = jnp.where(col >= keys_here, col - keys_here, col)
        return jnp.where(col <= diag + iota((rows, 1), 0), part, NEG)

    def peak_of(masked, s, n, top):
        for m in range(n * cols // LANES, (n + 1) * cols // LANES):
            part = masked_part(masked, s, m)
            top = part if top is None else jnp.maximum(top, part)
        return top

    def weigh(masked, s, peak, n, acc):
        parts = [
            jnp.exp2(masked_part(masked, s, m) - peak).astype(BF)
            for m in range(n * cols // LANES, (n + 1) * cols // LANES)
        ]
        w = jnp.concatenate(parts, axis=1)
        o = jnp.dot(w, vhat[pl.ds(n * cols, cols), :], preferred_element_type=F32)
        return o if acc is None else acc + o

    def store(p, h, o, peak):
        total = o[:, LANES:]
        head = p * 2 + h
        out[:, pl.ds(pl.multiple_of(head * LANES, LANES), LANES)] = (o[:, :LANES] / total).astype(BF)
        stat[...] = jnp.where(iota((rows, LANES), 1) == head, peak + jnp.log2(total), stat[...])

    ncol = keys_here // cols

    def half_step(masked, p, h, more, ahead):
        s, corr = (sa, ca) if h == 0 else (sb, cb)
        s2 = sb if h == 0 else sa
        steps = [functools.partial(scores, 2 * p + h + 1, s2, n) for n in range(ncol)] if more else []

        def one():
            if steps:
                steps.pop(0)()

        one()
        if masked:
            correct(s, corr)
        top = None
        for n in range(ncol):
            top = peak_of(masked, s, n, top)
        peak = jnp.max(top, axis=1, keepdims=True)
        one()
        acc = None
        for n in range(ncol):
            acc = weigh(masked, s, peak, n, acc)
            if n % 2:
                one()
        while steps:
            one()
        store(p, h, acc, peak)
        if masked and h == 0:
            correction(p, 1, cb)
            if ahead:
                future_band(p + 1)
        if masked and h == 1 and ahead:
            stack_band()
            correction(p + 1, 0, ca)

    def run(masked):
        if masked:
            win = kext[pl.ds(base + diag, nwin), :].astype(BF)
            flip = (iota((nwin, nwin), 0) + iota((nwin, nwin), 1) == nwin - 1).astype(F32).astype(BF)
            rev[...] = jnp.dot(flip, win, preferred_element_type=F32).astype(BF)
            fsc[:, 0:8, :] = jnp.zeros((2, 8, LANES), F32)
            msc[...] = jnp.zeros((2 * LANES, LANES), F32)
            future_band(0)
            stack_band()
            correction(0, 0, ca)
        for n in range(ncol):
            scores(0, sa, n)

        def body(p, c):
            half_step(masked, p, 0, True, True)
            half_step(masked, p, 1, True, True)
            return c

        if pairs > 1:
            lax.fori_loop(0, pairs - 1, body, 0)
        half_step(masked, pairs - 1, 0, True, False)
        half_step(masked, pairs - 1, 1, False, False)

    stat[...] = jnp.zeros((rows, LANES), F32)

    @pl.when(diag > keys_here + 8)
    def _():
        run(False)

    @pl.when(has_diag)
    def _():
        run(True)

    @pl.when(diag < 1 - rows)
    def _():
        out[...] = jnp.zeros_like(out)
        stat[...] = jnp.where(iota((rows, LANES), 1) < hk, NEG, 0.0)

    half = rows // 2
    side = lax.rem(seq // split_bit, 2)
    stats = pack_stats(stat[...], hk)
    stat[...] = stats
    for ref, part in ((keep_ref, side), (send_ref, 1 - side)):
        at = pl.multiple_of(part * half, half)
        ref[:, :hk * LANES] = out[pl.ds(at, half), :]
        ref[:, hk * LANES:] = stat[pl.ds(at, half), :].astype(BF)


def attend(kv, qtaps, offset, qhat, q2, k2, v2, from_pair, from_next, band):
    hk, rows, depth = qhat.shape
    kvs, keys_here, _ = k2.shape
    heads = hk * kvs
    page = from_pair.shape[0]
    ktaps = depth // LANES
    dims = (rows, heads, kvs, page, qtaps, ktaps, keys_here, 1)
    smem = pl.BlockSpec(memory_space=pltpu.SMEM)
    vmem = pl.BlockSpec(memory_space=pltpu.VMEM)
    width = hk * LANES + LANES
    shape = jax.ShapeDtypeStruct((rows // 2, width), BF)
    flops = 2 * hk * rows * keys_here * (ktaps + 2) * LANES
    return pl.pallas_call(
        functools.partial(attend_kernel, dims, kv),
        out_shape=(shape, shape),
        in_specs=[smem] + [vmem] * 7,
        out_specs=(vmem, vmem),
        scratch_shapes=[
            pltpu.VMEM((HEAD_PAD + keys_here + TAIL_PAD, LANES), F32),
            pltpu.VMEM((keys_here + 16, LANES), F32),
            pltpu.VMEM((LANES + 16, LANES), F32),
            pltpu.VMEM((keys_here + 2 * VPAD, LANES), F32),
            pltpu.VMEM((keys_here, ktaps * LANES), BF),
            pltpu.VMEM((keys_here, 2 * LANES), BF),
            pltpu.VMEM((rows, keys_here), F32),
            pltpu.VMEM((rows, keys_here), F32),
            pltpu.VMEM((rows, LANES), F32),
            pltpu.VMEM((rows, LANES), F32),
            pltpu.VMEM((rows, hk * LANES), BF),
            pltpu.VMEM((rows, LANES), F32),
            pltpu.VMEM((3 * LANES, LANES), BF),
            pltpu.VMEM((2, rows + 8, LANES), F32),
            pltpu.VMEM((rows, 2 * LANES), F32),
            pltpu.VMEM((2 * LANES, LANES), F32),
        ],
        compiler_params=pltpu.CompilerParams(vmem_limit_bytes=22 * 2**20),
        cost_estimate=pl.CostEstimate(flops=flops, bytes_accessed=4 * 2**20, transcendentals=hk * rows * keys_here),
        name=f"attend{kv}",
    )(offset, qhat, q2, k2, v2, from_pair, from_next, band)


def edge_kernel(table_ref, keys_ref, pair_ref, next_ref, sem):
    end = keys_ref.shape[0] - 1
    odd = lax.rem(lax.axis_index("seq"), 2)
    copies = [
        pltpu.make_async_copy(keys_ref.at[table_ref[p]], ref, sem.at[i])
        for i, (p, ref) in enumerate(((end * (1 - odd), pair_ref), (end * odd, next_ref)))
    ]
    for c in copies:
        c.start()
    for c in copies:
        c.wait()


def edge_pages(table, keys):
    one = jax.ShapeDtypeStruct(keys.shape[1:], keys.dtype)
    vmem = pl.BlockSpec(memory_space=pltpu.VMEM)
    return pl.pallas_call(
        edge_kernel,
        out_shape=(one, one),
        in_specs=[pl.BlockSpec(memory_space=pltpu.SMEM), pl.BlockSpec(memory_space=pltpu.HBM)],
        out_specs=(vmem, vmem),
        scratch_shapes=[pltpu.SemaphoreType.DMA((2,))],
        compiler_params=pltpu.CompilerParams(vmem_limit_bytes=2**20),
        cost_estimate=pl.CostEstimate(flops=2 * 10**10, bytes_accessed=2**20, transcendentals=0),
        name="edges",
    )(table, keys)


def place_in(level):
    seq = lax.axis_index("seq")
    place = 0
    for bit in level:
        place = place * 2 + lax.rem(seq // bit, 2)
    return place


def mask_of(level, rel):
    return sum(bit for i, bit in enumerate(reversed(level)) if rel >> i & 1)


def merge_kernel(hk, came, level, *refs):
    ins, outs = refs[:came], refs[came:]
    wide = hk * LANES
    lses = [unpack_stats(r[:, wide:], hk) for r in ins]
    top = functools.reduce(jnp.maximum, lses)
    lse = top + jnp.log2(sum(jnp.exp2(x - top) for x in lses))
    weights = [jnp.exp2(x - lse) for x in lses]
    rows = ins[0].shape[0]
    target = outs[-1] if level else outs[0]
    for h in range(hk):
        cols = slice(h * LANES, (h + 1) * LANES)
        mixed = sum(r[:, cols].astype(F32) * w[:, h:h + 1] for r, w in zip(ins, weights))
        target[:, cols] = mixed.astype(target.dtype)
    if level:
        target[:, wide:] = pack_stats(jnp.where(iota((rows, LANES), 1) < hk, lse, 0.0), hk)
        parts = 1 << len(level)
        size = rows // parts
        place = place_in(level)
        for rel in range(parts):
            at = pl.multiple_of(jnp.bitwise_xor(place, rel) * size, size)
            outs[rel][...] = target[pl.ds(at, size), :].astype(BF)


def merge(parts, hk, level):
    rows, width = parts[0].shape
    vmem = pl.BlockSpec(memory_space=pltpu.VMEM)
    if level:
        count = 1 << len(level)
        shapes = (jax.ShapeDtypeStruct((rows // count, width), BF),) * count
        specs = (vmem,) * count
        scratch = [pltpu.VMEM((rows, width), F32)]
    else:
        shapes, specs, scratch = jax.ShapeDtypeStruct((rows, hk * LANES), BF), vmem, []
    return pl.pallas_call(
        functools.partial(merge_kernel, hk, len(parts), level),
        out_shape=shapes,
        in_specs=[vmem] * len(parts),
        out_specs=specs,
        scratch_shapes=scratch,
        compiler_params=pltpu.CompilerParams(vmem_limit_bytes=4 * 2**20),
        cost_estimate=pl.CostEstimate(flops=4 * rows * width, bytes_accessed=6 * rows * width, transcendentals=rows * LANES * 5),
        name=f"merge{len(parts)}",
    )(*parts)


def project_kernel(chunks, heads_axis, *refs):
    xs = refs[:-4]
    w_ref, keep_ref, send_ref, xbuf = refs[-4:]
    count = lax.axis_size("seq")
    mine = place_in([1 << i for i in range(count.bit_length() - 1)])
    rows = xbuf.shape[0]
    unit = rows // count
    per = len(xs) // chunks
    width = xs[0].shape[1]
    for c in range(chunks):
        cols = slice(c * width, (c + 1) * width)
        held = 0
        for x_ref in xs[c * per:(c + 1) * per]:
            for k in range(x_ref.shape[0] // unit):
                to = jnp.bitwise_xor(mine, held)
                xbuf[pl.ds(pl.multiple_of(to * unit, unit), unit), cols] = (
                    x_ref[pl.ds(k * unit, unit), :].astype(xbuf.dtype))
                held += 1
    y = jnp.dot(xbuf[...].astype(BF), w_ref[...], preferred_element_type=F32)
    core = lax.rem(lax.axis_index("head"), 2)
    block = rows // heads_axis
    for g in range(heads_axis // 2):
        even = y[(2 * g) * block:(2 * g + 1) * block]
        odd = y[(2 * g + 1) * block:(2 * g + 2) * block]
        keep_ref[pl.ds(g * block, block), :] = jnp.where(core == 0, even, odd)
        send_ref[pl.ds(g * block, block), :] = jnp.where(core == 0, odd, even).astype(BF)


def project(chunks, pieces, weight, rows):
    heads_axis = lax.axis_size("head")
    vmem = pl.BlockSpec(memory_space=pltpu.VMEM)
    depth, cols = weight.shape
    unit = rows // lax.axis_size("seq")
    return pl.pallas_call(
        functools.partial(project_kernel, chunks, heads_axis),
        out_shape=(jax.ShapeDtypeStruct((rows // 2, cols), F32), jax.ShapeDtypeStruct((rows // 2, cols), BF)),
        in_specs=[vmem] * (len(pieces) + 1),
        out_specs=(vmem, vmem),
        scratch_shapes=[pltpu.VMEM((rows, depth), BF if unit % 16 == 0 else F32)],
        compiler_params=pltpu.CompilerParams(vmem_limit_bytes=12 * 2**20),
        cost_estimate=pl.CostEstimate(flops=2 * rows * depth * cols, bytes_accessed=2 * depth * cols, transcendentals=0),
        name="project",
    )(*pieces, weight)


def swap(x, axis, bit):
    count = lax.axis_size(axis)
    return lax.ppermute(x, axis, [(i, i ^ bit) for i in range(count)])


def per_device(queries, keys, values, page_table, offset, conv_kernel, head_mix, out_weight):
    rows, heads, head_dim = queries.shape
    pages, page, kvs, _ = keys.shape
    hk = heads // kvs
    seq_count = lax.axis_size("seq")
    head_count = lax.axis_size("head")

    to_pair, to_next = edge_pages(page_table, keys)
    from_pair = swap(to_pair, "seq", 1)
    from_next = lax.ppermute(
        to_next, "seq", [(i, j) for k in range(1, seq_count - 1, 2) for i, j in ((k, k + 1), (k + 1, k))])

    q2, k2, v2, band, *qhats = prepare(
        page_table, head_mix.T, jnp.transpose(conv_kernel, (2, 1, 0)), queries, keys, values)

    bits = [1 << i for i in range(seq_count.bit_length() - 1)]
    levels = [bits[:1]] + [bits[i:i + 2] for i in range(1, len(bits), 2)]
    pieces = []
    for kv in range(kvs):
        parts = attend(kv, conv_kernel.shape[1], offset, qhats[kv], q2, k2, v2, from_pair, from_next, band)
        for i, level in enumerate(levels):
            got = [swap(x, "seq", mask_of(level, rel)) for rel, x in enumerate(parts) if rel]
            parts = merge([parts[0], *got], hk, levels[i + 1] if i + 1 < len(levels) else None)
        held = [parts]
        for level in reversed(levels):
            whole = held[0] if len(held) == 1 else jnp.concatenate(held, axis=0)
            held += [swap(whole, "seq", mask_of(level, rel)) for rel in range(1, 1 << len(level))]
        pieces += held

    keep, send = project(kvs, pieces, out_weight, rows)
    me = lax.axis_index("head")
    got = swap(send, "head", 1)
    total = keep + got.astype(F32)
    block = rows // head_count
    bit = 2
    while bit < head_count:
        parts = total.reshape(-1, 2, block, total.shape[1])
        high = (me // bit) % 2 == 1
        mine = jnp.where(high, parts[:, 1], parts[:, 0])
        other = jnp.where(high, parts[:, 0], parts[:, 1]).astype(BF)
        got = swap(other, "head", bit)
        total = (mine + got.astype(F32)).reshape(-1, total.shape[1])
        bit *= 2
    return total.astype(BF)


def solution(mesh):
    placed = (
        P(None, "head", None),
        P("seq", None, "head", None),
        P("seq", None, "head", None),
        P("seq"),
        P(),
        P("head", None, None),
        P("head", None),
        P("head", "seq"),
    )
    return jax.shard_map(
        per_device, mesh=mesh, in_specs=placed, out_specs=P("head", "seq"), check_vma=False
    )
```
